32 devices in a mesh: grp: 4 (over x, core), dev: 8 (over z, y).
Axes of the slice: x: 2, y: 2, z: 4, core: 2. Of those that a mesh axis runs over, the one named last changes fastest.
Arguments:
- hot_table: float32 [2048, 768], P('dev'), may hold values from -6 to 6
- cold_table: float32 [32768, 768], P(('grp', 'dev')), may hold values from -6 to 6
- hot_need: int32 [256, 32], P(('grp', 'dev')), may hold values from -1 to 255, as said below
- cold_need: int32 [1024, 4], P(('grp', 'dev')), may hold values from -1 to 1023, as said below
- self_index: int32 [65536], P(('grp', 'dev')), may hold values from 0 to 383, as said below
- neighbors: int32 [65536, 25], P(('grp', 'dev')), may hold values from 0 to 383, as said below
- w_self: bfloat16 [768, 1024], replicated, may hold values from -0.21875 to 0.21875
- w_neigh: bfloat16 [768, 1024], replicated, may hold values from -1 to 1
- cotangent: bfloat16 [65536, 1024], P(('grp', 'dev')), may hold values from -0.0234375 to 0.0234375
Outputs:
- hidden: bfloat16 [65536, 1024], P(('grp', 'dev'))
- grad_self: float32 [768, 1024], replicated
- grad_neigh: float32 [768, 1024], replicated
The draws below stay inside these ranges and needn't reach their ends.
Inputs may be any that keep to these rules, and one draw needn't show every extreme that they name: `hot_need`: in each row the asked slots come first, 1 to 32 of them, then -1. In every draw some dev index is asked 32 slots by every device. `cold_need`: in each row the asked slots come first, 1 to 4 of them, then -1. In every draw some owner is asked 4 slots by every device. `self_index`: each entry names an asked slot of the device's own requests: p * 32 + k for the k-th hot slot asked of dev index p, or (devices along dev) * 32 + q * 4 + k for the k-th cold slot asked of owner q. `neighbors`: each entry names an asked slot of the device's own requests, numbered as for self_index.
All inputs are finite; a program needn't handle non-finite values.
Results may differ from the reference program's by a relative error of at most 0.0058.
Values sent between devices are 32-bit elements; how exact they have to be, the bound alone decides.
No kernel may reach another device: no remote copies, remote signals or barrier semaphores. Data moves between devices by JAX's collectives and lax.ppermute only.
A program may use at most 192 MiB of HBM per device.

```python
import jax
import jax.numpy as jnp
from jax import lax

D = 768
H = 1024
FAN = 25
TGT = 2048
HCAP = 32
CCAP = 4
HOT_DEV = 256
COLD_DEV = 1024
HOT = 2048
COLD = 32768
N_DEV = 8
DEVICES = 32


def need_counts(key, peer_count, capacity, salt_value):
    local_key = jax.random.fold_in(key, salt_value)
    counts = jax.random.randint(local_key, (DEVICES, peer_count), 1, capacity + 1)
    full_peer = jax.random.randint(jax.random.fold_in(local_key, 1), (), 0, peer_count)
    return jnp.where(jnp.arange(peer_count)[None, :] == full_peer, capacity, counts)


def asked_lists(key, counts, capacity, shard_rows):
    slots = jax.random.randint(key, counts.shape + (capacity,), 0, shard_rows)
    valid = jnp.arange(capacity)[None, None, :] < counts[:, :, None]
    return jnp.where(valid, slots, -1).reshape(-1, capacity).astype(jnp.int32)


def source_positions(key, hot_counts, cold_counts, out_shape):
    subkeys = jax.random.split(key, 5)
    full_shape = (DEVICES,) + out_shape
    which_kind = jax.random.randint(subkeys[0], full_shape, 0, 2)
    hot_peer = jax.random.randint(subkeys[1], full_shape, 0, N_DEV)
    cold_peer = jax.random.randint(subkeys[2], full_shape, 0, DEVICES)
    device_ids = jnp.arange(DEVICES).reshape((DEVICES,) + (1,) * len(out_shape))
    hot_limit = hot_counts[device_ids, hot_peer]
    cold_limit = cold_counts[device_ids, cold_peer]
    hot_pick = jax.random.randint(subkeys[3], full_shape, 0, hot_limit)
    cold_pick = jax.random.randint(subkeys[4], full_shape, 0, cold_limit)
    hot_slot = hot_peer * HCAP + hot_pick
    cold_slot = N_DEV * HCAP + cold_peer * CCAP + cold_pick
    return jnp.where(which_kind == 0, hot_slot, cold_slot).astype(jnp.int32)


def draw_hot_need(key, part):
    counts = need_counts(key, N_DEV, HCAP, 11)
    key = jax.random.fold_in(key, 3)
    return asked_lists(key, counts, HCAP, HOT_DEV)


def draw_cold_need(key, part):
    counts = need_counts(key, DEVICES, CCAP, 12)
    key = jax.random.fold_in(key, 4)
    return asked_lists(key, counts, CCAP, COLD_DEV)


def draw_self_index(key, part):
    hot_counts = need_counts(key, N_DEV, HCAP, 11)
    cold_counts = need_counts(key, DEVICES, CCAP, 12)
    key = jax.random.fold_in(key, 5)
    return source_positions(key, hot_counts, cold_counts, (TGT,)).reshape(DEVICES * TGT)


def draw_neighbors(key, part):
    hot_counts = need_counts(key, N_DEV, HCAP, 11)
    cold_counts = need_counts(key, DEVICES, CCAP, 12)
    key = jax.random.fold_in(key, 7)
    return source_positions(key, hot_counts, cold_counts, (TGT, FAN)).reshape(DEVICES * TGT, FAN)


def level_of(own_key, shape, cuts, low, top_value):
    def one(dim, blocks):
        draws = jax.random.uniform(jax.random.fold_in(jax.random.fold_in(own_key, 6), dim), (blocks,), jnp.float32, low / len(cuts), top_value / len(cuts))
        return jnp.repeat(jnp.exp(draws), shape[dim] // blocks).reshape((-1,) + (1,) * (len(shape) - dim - 1))

    loudness = one(*cuts[0])
    for cut in cuts[1:]:
        loudness = loudness * one(*cut)
    return loudness


def gaussian(own_key, dims, width, reach, cuts=(), held_as=jnp.bfloat16):
    array = jax.random.normal(own_key, dims, jnp.float32) * width
    if len(cuts) > 0:
        array = level_of(own_key, dims, cuts, -0.22, 0.18) * array
    return jnp.clip(array, min=-reach, max=reach).astype(held_as)


def setup_inputs(seed: int = 0) -> dict:
    seeds = jax.random.split(jax.random.key(seed), 10)
    hot_table = gaussian(seeds[0], (HOT, D), 1.0, 6.0, ((0, 8),), jnp.float32)
    cold_table = gaussian(seeds[1], (COLD, D), 1.0, 6.0, ((0, 32),), jnp.float32)
    hot_need = draw_hot_need(jax.random.fold_in(seeds[9], 71), 0)
    cold_need = draw_cold_need(jax.random.fold_in(seeds[9], 71), 0)
    self_index = draw_self_index(jax.random.fold_in(seeds[9], 71), 0)
    neighbors = draw_neighbors(jax.random.fold_in(seeds[9], 71), 0)
    w_self = gaussian(seeds[6], (D, H), D ** -0.5, 0.21875)
    w_neigh = gaussian(seeds[7], (D, H), (D // FAN) ** -0.5, 1.0)
    cotangent = gaussian(seeds[8], (DEVICES * TGT, H), (TGT * DEVICES) ** -0.5, 0.0234375, ((0, 32),))
    return dict(hot_table=hot_table, cold_table=cold_table, hot_need=hot_need, cold_need=cold_need, self_index=self_index, neighbors=neighbors, w_self=w_self, w_neigh=w_neigh, cotangent=cotangent)


def fetch_rows(feature_table, asked_slots, shard_rows):
    peer_count = asked_slots.shape[0]
    offsets = (jnp.arange(peer_count, dtype=jnp.int32) * shard_rows)[:, None]
    picked = jnp.take(feature_table, jnp.maximum(asked_slots, 0) + offsets, axis=0)
    present = (asked_slots >= 0)[..., None].astype(picked.dtype)
    return (picked * present).reshape(-1, feature_table.shape[1])


def reference(hot_table, cold_table, hot_need, cold_need, self_index, neighbors, w_self, w_neigh, cotangent):
    hot_all = hot_need.reshape(DEVICES, N_DEV, HCAP)
    cold_all = cold_need.reshape(DEVICES, DEVICES, CCAP)
    self_all = self_index.reshape(DEVICES, TGT)
    neigh_all = neighbors.reshape(DEVICES, TGT, FAN)
    cot_all = cotangent.reshape(DEVICES, TGT, H)

    def device_step(totals, inputs):
        hot_lists, cold_lists, self_slots, neigh_slots, cot_rows = inputs
        sources = jnp.concatenate([fetch_rows(hot_table, hot_lists, HOT_DEV), fetch_rows(cold_table, cold_lists, COLD_DEV)], axis=0)
        self_feat = jnp.take(sources, self_slots, axis=0).astype(jnp.bfloat16)
        neigh_feat = (jnp.sum(jnp.take(sources, neigh_slots, axis=0), axis=1) / FAN).astype(jnp.bfloat16)
        pre_act = jnp.dot(self_feat, w_self, preferred_element_type=jnp.float32) + jnp.dot(neigh_feat, w_neigh, preferred_element_type=jnp.float32)
        sigma = jax.nn.sigmoid(pre_act)
        hidden = (pre_act * sigma).astype(jnp.bfloat16)
        slope = sigma * (1.0 + pre_act * (1.0 - sigma))
        masked = (cot_rows.astype(jnp.float32) * slope).astype(jnp.bfloat16)
        grad_self = totals[0] + jnp.dot(self_feat.T, masked, preferred_element_type=jnp.float32)
        grad_neigh = totals[1] + jnp.dot(neigh_feat.T, masked, preferred_element_type=jnp.float32)
        return (grad_self, grad_neigh), hidden

    zero_grads = (jnp.zeros((D, H), jnp.float32), jnp.zeros((D, H), jnp.float32))
    totals, hidden = lax.scan(device_step, zero_grads, (hot_all, cold_all, self_all, neigh_all, cot_all))
    return hidden.reshape(DEVICES * TGT, H), totals[0], totals[1]
```

```python
import functools

import jax
import jax.numpy as jnp
from jax import lax
from jax.experimental import pallas as pl
from jax.experimental.pallas import tpu as pltpu
from jax.sharding import PartitionSpec as P

FAN = 25
CORES = 2
CHUNKS = 4
VMEM_LIMIT = 48 * 1024 * 1024


def look_up(feature_table, requests):
    picked = jnp.take(feature_table, jnp.maximum(requests, 0), axis=0)
    return picked * (requests >= 0)[..., None].astype(jnp.float32)


def count_kernel(slots_ref, self_ref, x_ref, xt_ref):
    rows, n_src = x_ref.shape[0], x_ref.shape[1] // 2
    step = 64

    @pl.loop(0, rows // step)
    def _(i):
        here = pl.ds(pl.multiple_of(i * step, step), step)
        lanes = lax.broadcasted_iota(jnp.int32, (step, n_src), 1)
        slots = slots_ref[here, :]
        total = jnp.zeros((step, n_src), jnp.float32)
        for j in range(FAN):
            total += jnp.where(slots[:, j : j + 1] == lanes, 1.0, 0.0)
        x_ref[here, pl.ds(n_src, n_src)] = total.astype(jnp.bfloat16)
        own = jnp.where(self_ref[here, :] == lanes, 1.0, 0.0)
        x_ref[here, pl.ds(0, n_src)] = own.astype(jnp.bfloat16)

    xt_ref[...] = x_ref[...].astype(jnp.float32).T.astype(jnp.bfloat16)


def count_matrices(neighbors, self_index, n_src):
    targets = neighbors.shape[0]
    block = 256
    return pl.pallas_call(
        count_kernel,
        grid=(targets // block,),
        in_specs=[
            pl.BlockSpec((block, FAN), lambda i: (i, 0)),
            pl.BlockSpec((block, 1), lambda i: (i, 0)),
        ],
        out_specs=[
            pl.BlockSpec((block, 2 * n_src), lambda i: (i, 0)),
            pl.BlockSpec((2 * n_src, block), lambda i: (0, i)),
        ],
        out_shape=[
            jax.ShapeDtypeStruct((targets, 2 * n_src), jnp.bfloat16),
            jax.ShapeDtypeStruct((2 * n_src, targets), jnp.bfloat16),
        ],
        compiler_params=pltpu.CompilerParams(vmem_limit_bytes=VMEM_LIMIT),
        cost_estimate=pl.CostEstimate(
            flops=2 * targets * n_src * FAN, bytes_accessed=4 * targets * n_src * 2, transcendentals=0
        ),
        name="count_matrices",
    )(neighbors, self_index[:, None])


def layer_kernel(
    core_ref, x_ref, xt_ref, hot_ref, cold_ref, w_self_ref, w_neigh_ref, cot_ref, *rest
):
    hidden_ref, keep_ref, send_ref, src, src_t, prod, back = rest[-7:]
    n_hot, n_src = hot_ref.shape[0], src.shape[0]
    step = pl.program_id(0)

    @pl.when(step == 0)
    def _():
        src[:n_hot, :] = hot_ref[...].astype(jnp.bfloat16)
        src[n_hot:, :] = cold_ref[...].astype(jnp.bfloat16)
        src_t[...] = jnp.concatenate([hot_ref[...], cold_ref[...]], axis=0).T.astype(jnp.bfloat16)
        prod[:n_src, :] = jnp.dot(
            src[...], w_self_ref[...], preferred_element_type=jnp.float32
        ).astype(jnp.bfloat16)
        prod[n_src:, :] = (
            jnp.dot(src[...], w_neigh_ref[...], preferred_element_type=jnp.float32) * (1.0 / FAN)
        ).astype(jnp.bfloat16)
        back[...] = jnp.zeros_like(back)

    pre_act = jnp.dot(x_ref[...], prod[...], preferred_element_type=jnp.float32)
    sigma = jax.nn.sigmoid(pre_act)
    hidden_ref[...] = (pre_act * sigma).astype(jnp.bfloat16)
    slope = sigma * (1.0 + pre_act * (1.0 - sigma))
    masked = (cot_ref[...].astype(jnp.float32) * slope).astype(jnp.bfloat16)
    back[0] += jnp.dot(xt_ref[:n_src, :], masked, preferred_element_type=jnp.float32)
    back[1] += jnp.dot(xt_ref[n_src:, :], masked, preferred_element_type=jnp.float32)

    @pl.when(step == pl.num_programs(0) - 1)
    def _():
        core = core_ref[0]
        for which, out_ref in ((core, keep_ref), (1 - core, send_ref)):
            scale = jnp.where(which == 0, 1.0, 1.0 / FAN)
            term = (back[which] * scale).astype(jnp.bfloat16)
            out_ref[...] = jnp.dot(src_t[...], term, preferred_element_type=jnp.float32)


def layer_chunk(chunk, core, x, xt, hot_rows, cold_rows, w_self, w_neigh, cotangent, hidden):
    targets, hidden_units = cotangent.shape
    feat_width = w_self.shape[0]
    n_src = x.shape[1] // 2
    cols = hidden_units // CHUNKS
    block = 512
    whole = lambda i, c: (0, 0)
    column = lambda i, c: (0, chunk)
    tile = lambda i, c: (i, chunk)
    in_specs = [
        pl.BlockSpec((block, 2 * n_src), lambda i, c: (i, 0)),
        pl.BlockSpec((2 * n_src, block), lambda i, c: (0, i)),
        pl.BlockSpec(hot_rows.shape, whole),
        pl.BlockSpec(cold_rows.shape, whole),
        pl.BlockSpec((feat_width, cols), column),
        pl.BlockSpec((feat_width, cols), column),
        pl.BlockSpec((block, cols), tile),
    ]
    operands = [core, x, xt, hot_rows, cold_rows, w_self, w_neigh, cotangent]
    aliases = {}
    if hidden is not None:
        in_specs.append(pl.BlockSpec(memory_space=pl.ANY))
        operands.append(hidden)
        aliases = {8: 0}
    return pl.pallas_call(
        layer_kernel,
        grid_spec=pltpu.PrefetchScalarGridSpec(
            num_scalar_prefetch=1,
            grid=(targets // block,),
            in_specs=in_specs,
            out_specs=[
                pl.BlockSpec((block, cols), tile),
                pl.BlockSpec((feat_width, cols), whole),
                pl.BlockSpec((feat_width, cols), whole),
            ],
            scratch_shapes=[
                pltpu.VMEM((n_src, feat_width), jnp.bfloat16),
                pltpu.VMEM((feat_width, n_src), jnp.bfloat16),
                pltpu.VMEM((2 * n_src, cols), jnp.bfloat16),
                pltpu.VMEM((2, n_src, cols), jnp.float32),
            ],
        ),
        out_shape=[
            jax.ShapeDtypeStruct((targets, hidden_units), jnp.bfloat16),
            jax.ShapeDtypeStruct((feat_width, cols), jnp.float32),
            jax.ShapeDtypeStruct((feat_width, cols), jnp.float32),
        ],
        input_output_aliases=aliases,
        compiler_params=pltpu.CompilerParams(vmem_limit_bytes=VMEM_LIMIT),
        cost_estimate=pl.CostEstimate(
            flops=4 * n_src * cols * (2 * targets + 2 * feat_width),
            bytes_accessed=8 * targets * n_src + 4 * targets * cols,
            transcendentals=targets * cols,
        ),
        name=f"layer_chunk_{chunk}",
    )(*operands)


class Line:
    def __init__(self, name, size, inner):
        self.name, self.size, self.inner = name, size, inner
        self.total = lax.axis_size(name)
        self.me = lax.rem(lax.div(lax.axis_index(name), jnp.int32(inner)), jnp.int32(size))

    def other(self, shift):
        return lax.rem(self.me + shift, jnp.int32(self.size))

    def send(self, value, shift):
        pairs = []
        for i in range(self.total):
            low, mine, high = i % self.inner, i // self.inner % self.size, i // (self.inner * self.size)
            to = (high * self.size + (mine + shift) % self.size) * self.inner + low
            pairs.append((i, to))
        return lax.ppermute(value, self.name, pairs)


def part(value, index, rows):
    return lax.dynamic_slice_in_dim(value, index * rows, rows, axis=0)


def scatter_sum(terms, line):
    rows = terms[0].shape[0] // line.size
    mine = [part(t, line.me, rows) for t in terms]
    for shift in range(1, line.size):
        out = functools.reduce(jnp.add, [part(t, line.other(shift), rows) for t in terms])
        mine.append(line.send(out, shift))
    return mine


def gather(value, line):
    rows = value.shape[0]
    whole = jnp.zeros((line.size * rows,) + value.shape[1:], value.dtype)
    whole = lax.dynamic_update_slice_in_dim(whole, value, line.me * rows, axis=0)
    for shift in range(1, line.size):
        got = line.send(value, shift)
        origin = lax.rem(line.me + line.size - shift, jnp.int32(line.size))
        whole = lax.dynamic_update_slice_in_dim(whole, got, origin * rows, axis=0)
    return whole


def body(
    hot_table, cold_table, hot_need, cold_need, self_index, neighbors, w_self, w_neigh, cotangent
):
    feat_width = hot_table.shape[1]
    both = ("grp", "dev")
    n_src = hot_need.size + cold_need.size
    x, xt = count_matrices(neighbors, self_index, n_src)

    swap = functools.partial(lax.all_to_all, split_axis=0, concat_axis=0, tiled=True)
    hot_rows = swap(look_up(hot_table, swap(hot_need, "dev")), "dev").reshape(-1, feat_width)
    cold_rows = swap(look_up(cold_table, swap(cold_need, both)), both).reshape(-1, feat_width)

    grp_size, dev_size = lax.axis_size("grp"), lax.axis_size("dev")
    x_size = grp_size // CORES
    y_size = x_size if dev_size % x_size == 0 else 1
    core = Line("grp", CORES, 1)
    along_x = Line("grp", x_size, CORES)
    along_y = Line("dev", y_size, 1)
    along_z = Line("dev", dev_size // y_size, y_size)

    hidden = None
    grads = []
    for chunk in range(CHUNKS):
        hidden, keep, send = layer_chunk(
            chunk, core.me[None], x, xt, hot_rows, cold_rows, w_self, w_neigh, cotangent, hidden
        )
        order = (along_x, along_y, along_z) if chunk % 2 == 0 else (along_y, along_x, along_z)
        terms = [keep, core.send(send, 1)]
        for line in order:
            terms = scatter_sum(terms, line)
        value = functools.reduce(jnp.add, terms)
        for line in reversed(order):
            value = gather(value, line)
        grads.append((value, core.send(value, 1)))
    own = jnp.concatenate([g[0] for g in grads], axis=1)
    other = jnp.concatenate([g[1] for g in grads], axis=1)
    first = core.me == 0
    return (hidden, jnp.where(first, own, other), jnp.where(first, other, own))


def solution(mesh):
    in_specs = (
        P("dev", None),
        P(("grp", "dev"), None),
        P(("grp", "dev"), None),
        P(("grp", "dev"), None),
        P(("grp", "dev")),
        P(("grp", "dev"), None),
        P(),
        P(),
        P(("grp", "dev"), None),
    )
    out_specs = (P(("grp", "dev"), None), P(), P())
    return jax.shard_map(body, mesh=mesh, in_specs=in_specs, out_specs=out_specs, check_vma=False)
```

```python
import functools

import jax
import jax.numpy as jnp
from jax import lax
from jax.experimental import pallas as pl
from jax.experimental.pallas import tpu as pltpu
from jax.sharding import PartitionSpec as P

FAN = 25
CORES = 2
CHUNKS = 4
CALLS = 2
VMEM_LIMIT = 48 * 1024 * 1024


def look_up(feature_table, requests):
    picked = jnp.take(feature_table, jnp.maximum(requests, 0), axis=0)
    return picked * (requests >= 0)[..., None].astype(jnp.float32)


def split(value):
    high = value.astype(jnp.bfloat16)
    return high, (value - high.astype(jnp.float32)).astype(jnp.bfloat16)


def dot(left, right):
    return jnp.dot(left, right, preferred_element_type=jnp.float32)


def dot_rows(left, right):
    return lax.dot_general(
        left, right, (((0,), (0,)), ((), ())), preferred_element_type=jnp.float32
    )


def count_kernel(slots_ref, self_ref, counts_ref):
    n_src, targets = counts_ref.shape[0] // 2, counts_ref.shape[1]
    step = 32
    slots = slots_ref[...].astype(jnp.int16)
    own = self_ref[...].astype(jnp.int16)

    @pl.loop(0, n_src // step)
    def _(i):
        base = pl.multiple_of(i * step, step)
        ids = (lax.broadcasted_iota(jnp.int32, (step, targets), 0) + base).astype(jnp.int16)
        one = jnp.ones((step, targets), jnp.bfloat16)
        zero = jnp.zeros((step, targets), jnp.bfloat16)
        total = zero
        for j in range(FAN):
            total += jnp.where(slots[j : j + 1, :] == ids, one, zero)
        counts_ref[pl.ds(n_src + base, step), :] = total
        counts_ref[pl.ds(base, step), :] = jnp.where(own == ids, one, zero)


def count_matrices(neighbors, self_index, n_src):
    targets = neighbors.shape[0]
    block = 512
    return pl.pallas_call(
        count_kernel,
        grid=(targets // block,),
        in_specs=[
            pl.BlockSpec((FAN, block), lambda i: (0, i)),
            pl.BlockSpec((1, block), lambda i: (0, i)),
        ],
        out_specs=pl.BlockSpec((2 * n_src, block), lambda i: (0, i)),
        out_shape=jax.ShapeDtypeStruct((2 * n_src, targets), jnp.bfloat16),
        compiler_params=pltpu.CompilerParams(vmem_limit_bytes=VMEM_LIMIT),
        cost_estimate=pl.CostEstimate(
            flops=2 * targets * n_src * FAN, bytes_accessed=4 * targets * n_src, transcendentals=0
        ),
        name="count_matrices",
    )(neighbors.T, self_index[None, :])


def layer_kernel(
    chunks, core_ref, counts_ref, hot_ref, cold_ref, w_self_ref, w_neigh_ref, cot_ref, *rest
):
    src, prod, back = rest[-3:]
    grad_refs = rest[-3 - 2 * chunks : -3]
    hidden_ref = rest[-4 - 2 * chunks]
    n_hot, n_src = hot_ref.shape[0], src.shape[1]
    step = pl.program_id(0)

    @pl.when(step == 0)
    def _():
        src[0, :n_hot, :], src[1, :n_hot, :] = split(hot_ref[...])
        src[0, n_hot:, :], src[1, n_hot:, :] = split(cold_ref[...])
        prod[:n_src, :] = dot(src[0], w_self_ref[...]).astype(jnp.bfloat16)
        both = dot(src[0], w_neigh_ref[...]) + dot(src[1], w_neigh_ref[...])
        prod[n_src:, :] = (both * (1.0 / FAN)).astype(jnp.bfloat16)
        back[...] = jnp.zeros_like(back)

    pre_act = dot_rows(counts_ref[...], prod[...])
    sigma = 0.5 * jnp.tanh(0.5 * pre_act) + 0.5
    hidden_ref[...] = (pre_act * sigma).astype(jnp.bfloat16)
    slope = sigma * (1.0 + pre_act * (1.0 - sigma))
    masked = (cot_ref[...].astype(jnp.float32) * slope).astype(jnp.bfloat16)
    back[...] += dot(counts_ref[...], masked)

    @pl.when(step == pl.num_programs(0) - 1)
    def _():
        cols = back.shape[1] // chunks

        def self_term(part):
            high, low = split(back[:n_src, pl.ds(part * cols, cols)])
            return dot_rows(src[0], high) + dot_rows(src[0], low)

        def neigh_term(part):
            high, low = split(back[n_src:, pl.ds(part * cols, cols)] * (1.0 / FAN))
            return dot_rows(src[0], high) + dot_rows(src[0], low) + dot_rows(src[1], high)

        @pl.when(core_ref[0] == 0)
        def _():
            for part in range(chunks):
                grad_refs[2 * part][...] = self_term(part)
                grad_refs[2 * part + 1][...] = neigh_term(part)

        @pl.when(core_ref[0] != 0)
        def _():
            for part in range(chunks):
                grad_refs[2 * part][...] = neigh_term(part)
                grad_refs[2 * part + 1][...] = self_term(part)


def layer(call, chunks, core, counts, hot_rows, cold_rows, w_self, w_neigh, cotangent, hidden):
    targets, hidden_units = cotangent.shape
    feat_width = w_self.shape[0]
    n_src = counts.shape[0] // 2
    wide = hidden_units // CALLS
    cols = wide // chunks
    block = 512
    whole = lambda i, c: (0, 0)
    column = lambda i, c: (0, call)
    tile = lambda i, c: (i, call)
    in_specs = [
        pl.BlockSpec((2 * n_src, block), lambda i, c: (0, i)),
        pl.BlockSpec(hot_rows.shape, whole),
        pl.BlockSpec(cold_rows.shape, whole),
        pl.BlockSpec((feat_width, wide), column),
        pl.BlockSpec((feat_width, wide), column),
        pl.BlockSpec((block, wide), tile),
    ]
    operands = [core, counts, hot_rows, cold_rows, w_self, w_neigh, cotangent]
    aliases = {}
    if hidden is not None:
        in_specs.append(pl.BlockSpec(memory_space=pl.ANY))
        operands.append(hidden)
        aliases = {7: 0}
    return pl.pallas_call(
        functools.partial(layer_kernel, chunks),
        grid_spec=pltpu.PrefetchScalarGridSpec(
            num_scalar_prefetch=1,
            grid=(targets // block,),
            in_specs=in_specs,
            out_specs=[pl.BlockSpec((block, wide), tile)]
            + [pl.BlockSpec((feat_width, cols), whole)] * (2 * chunks),
            scratch_shapes=[
                pltpu.VMEM((2, n_src, feat_width), jnp.bfloat16),
                pltpu.VMEM((2 * n_src, wide), jnp.bfloat16),
                pltpu.VMEM((2 * n_src, wide), jnp.float32),
            ],
        ),
        out_shape=[jax.ShapeDtypeStruct((targets, hidden_units), jnp.bfloat16)]
        + [jax.ShapeDtypeStruct((feat_width, cols), jnp.float32)] * (2 * chunks),
        input_output_aliases=aliases,
        compiler_params=pltpu.CompilerParams(vmem_limit_bytes=VMEM_LIMIT),
        cost_estimate=pl.CostEstimate(
            flops=4 * n_src * wide * (2 * targets + 2 * feat_width),
            bytes_accessed=4 * targets * n_src + 4 * targets * wide,
            transcendentals=targets * wide,
        ),
        name=f"layer_{call}",
    )(*operands)


def place_kernel(where_ref, mine, got, other_mine, other_got, *rest):
    out_self, out_neigh = rest[-2:]
    mine_here = pl.program_id(0) == where_ref[1]
    first_core = where_ref[0] == 0
    for here, own, other in ((mine_here, mine, other_mine), (~mine_here, got, other_got)):

        @pl.when(here & first_core)
        def _(own=own, other=other):
            out_self[...] = own[...]
            out_neigh[...] = other[...]

        @pl.when(here & ~first_core)
        def _(own=own, other=other):
            out_self[...] = other[...]
            out_neigh[...] = own[...]


def place(chunk, where, pieces, outs):
    rows, cols = pieces[0].shape
    shape = jax.ShapeDtypeStruct((2 * rows, CHUNKS * cols), jnp.float32)
    return pl.pallas_call(
        place_kernel,
        grid_spec=pltpu.PrefetchScalarGridSpec(
            num_scalar_prefetch=1,
            grid=(2,),
            in_specs=[pl.BlockSpec((rows, cols), lambda i, w: (0, 0))] * 4
            + [pl.BlockSpec(memory_space=pl.ANY)] * len(outs),
            out_specs=[pl.BlockSpec((rows, cols), lambda i, w: (i, chunk))] * 2,
        ),
        out_shape=[shape, shape],
        input_output_aliases={5: 0, 6: 1} if outs else {},
        compiler_params=pltpu.CompilerParams(vmem_limit_bytes=VMEM_LIMIT),
        cost_estimate=pl.CostEstimate(flops=0, bytes_accessed=32 * rows * cols, transcendentals=0),
        name=f"place_chunk_{chunk}",
    )(where, *pieces, *outs)


class Swap:
    def __init__(self, name, mask, bit):
        self.name, self.mask, self.bit = name, mask, bit
        self.pairs = [(i, i ^ mask) for i in range(lax.axis_size(name))]

    def send(self, value):
        return lax.ppermute(value, self.name, self.pairs)


def swaps(name, stride, size):
    index = lax.axis_index(name)
    found = []
    step = 1
    while step < size:
        low = lax.rem(lax.div(index, jnp.int32(stride * step)), jnp.int32(2))
        high = lax.rem(lax.div(index, jnp.int32(stride * step * 2)), jnp.int32(2)) if 2 * step < size else 0
        found.append(Swap(name, stride * (2 * step - 1), lax.rem(low + high, jnp.int32(2))))
        step *= 2
    return found


def halve(terms, swap):
    rows = terms[0].shape[0] // 2
    low = functools.reduce(jnp.add, [t[:rows] for t in terms])
    high = functools.reduce(jnp.add, [t[rows:] for t in terms])
    out = jnp.where(swap.bit == 0, high, low)
    return [jnp.where(swap.bit == 0, low, high), swap.send(out)]


def double(value, swap):
    got = swap.send(value)
    first = swap.bit == 0
    return jnp.concatenate([jnp.where(first, value, got), jnp.where(first, got, value)], axis=0)


def sum_over_devices(terms, core):
    groups, dev_size = lax.axis_size("grp"), lax.axis_size("dev")
    x_size = groups // CORES
    y_size = x_size if dev_size % x_size == 0 else 1
    along_x = swaps("grp", CORES, x_size)
    along_y = swaps("dev", 1, y_size)
    along_z = swaps("dev", y_size, dev_size // y_size)
    near_z, far_z = along_z[:1], along_z[1:]
    orders = [
        along_x + along_y + near_z + far_z,
        along_y + along_x + near_z + far_z,
        near_z + along_x + along_y + far_z,
        along_y + along_x + near_z + far_z,
    ]
    grads = []
    for chunk, (keep, send) in enumerate(terms):
        order = orders[chunk]
        parts = [keep, core.send(send)]
        for swap in order[:-1]:
            parts = halve(parts, swap)
        value = parts[0] + parts[1]
        value = value + order[-1].send(value)
        for swap in order[-2:0:-1]:
            value = double(value, swap)
        got = order[0].send(value)
        where = jnp.stack([core.bit, order[0].bit]).astype(jnp.int32)
        grads = place(chunk, where, [value, got, core.send(value), core.send(got)], grads)
    return grads


def body(
    hot_table, cold_table, hot_need, cold_need, self_index, neighbors, w_self, w_neigh, cotangent
):
    feat_width = hot_table.shape[1]
    both = ("grp", "dev")
    n_src = hot_need.size + cold_need.size
    counts = count_matrices(neighbors, self_index, n_src)

    exchange = functools.partial(
        lax.all_to_all, axis_name=both, split_axis=0, concat_axis=0, tiled=True
    )
    groups, dev_size = lax.axis_size("grp"), lax.axis_size("dev")
    cold_slots = cold_need.shape[1]
    asked = exchange(jnp.concatenate([cold_need, jnp.tile(hot_need, (groups, 1))], axis=1))
    cold_asked = asked[:, :cold_slots]
    hot_asked = lax.dynamic_slice_in_dim(
        asked[:, cold_slots:], lax.axis_index("grp") * dev_size, dev_size, axis=0
    )
    cold_rows = exchange(look_up(cold_table, cold_asked)).reshape(-1, feat_width)
    hot_rows = lax.all_to_all(
        look_up(hot_table, hot_asked), "dev", split_axis=0, concat_axis=0, tiled=True
    ).reshape(-1, feat_width)

    core = swaps("grp", 1, CORES)[0]
    hidden = None
    terms = []
    for call in range(CALLS):
        hidden, *grads = layer(
            call, CHUNKS // CALLS, core.bit[None], counts, hot_rows, cold_rows, w_self, w_neigh, cotangent, hidden
        )
        terms += list(zip(grads[::2], grads[1::2]))
    grad_self, grad_neigh = sum_over_devices(terms, core)
    return (hidden, grad_self, grad_neigh)


def solution(mesh):
    in_specs = (
        P("dev", None),
        P(("grp", "dev"), None),
        P(("grp", "dev"), None),
        P(("grp", "dev"), None),
        P(("grp", "dev")),
        P(("grp", "dev"), None),
        P(),
        P(),
        P(("grp", "dev"), None),
    )
    out_specs = (P(("grp", "dev"), None), P(), P())
    return jax.shard_map(body, mesh=mesh, in_specs=in_specs, out_specs=out_specs, check_vma=False)
```

```python
import functools

import jax
import jax.numpy as jnp
from jax import lax
from jax.experimental import pallas as pl
from jax.experimental.pallas import tpu as pltpu
from jax.sharding import PartitionSpec as P

FAN = 25
CORES = 2
CHUNKS = 4
CALLS = 2
VMEM_LIMIT = 48 * 1024 * 1024


def split(value):
    high = value.astype(jnp.bfloat16)
    return high, (value - high.astype(jnp.float32)).astype(jnp.bfloat16)


def dot(left, right):
    return jnp.dot(left, right, preferred_element_type=jnp.float32)


def dot_rows(left, right):
    return lax.dot_general(
        left, right, (((0,), (0,)), ((), ())), preferred_element_type=jnp.float32
    )


def count_kernel(slots_ref, self_ref, counts_ref):
    n_src, targets = counts_ref.shape[0] // 2, counts_ref.shape[1]
    step = 32
    slots = slots_ref[...].astype(jnp.int16)
    own = self_ref[...].astype(jnp.int16)

    @pl.loop(0, n_src // step)
    def _(i):
        base = pl.multiple_of(i * step, step)
        ids = (lax.broadcasted_iota(jnp.int32, (step, targets), 0) + base).astype(jnp.int16)
        one = jnp.ones((step, targets), jnp.bfloat16)
        zero = jnp.zeros((step, targets), jnp.bfloat16)
        total = zero
        for j in range(FAN):
            total += jnp.where(slots[j : j + 1, :] == ids, one, zero)
        counts_ref[pl.ds(n_src + base, step), :] = total
        counts_ref[pl.ds(base, step), :] = jnp.where(own == ids, one, zero)


def count_matrices(neighbors, self_index, n_src):
    targets = neighbors.shape[0]
    block = 512
    return pl.pallas_call(
        count_kernel,
        grid=(targets // block,),
        in_specs=[
            pl.BlockSpec((FAN, block), lambda i: (0, i)),
            pl.BlockSpec((1, block), lambda i: (0, i)),
        ],
        out_specs=pl.BlockSpec((2 * n_src, block), lambda i: (0, i)),
        out_shape=jax.ShapeDtypeStruct((2 * n_src, targets), jnp.bfloat16),
        compiler_params=pltpu.CompilerParams(vmem_limit_bytes=VMEM_LIMIT),
        cost_estimate=pl.CostEstimate(
            flops=2 * targets * n_src * FAN, bytes_accessed=4 * targets * n_src, transcendentals=0
        ),
        name="count_matrices",
    )(neighbors.T, self_index[None, :])


def pick(rows_named, table):
    ids = lax.broadcasted_iota(jnp.int32, (table.shape[0], rows_named.shape[1]), 0)
    chosen = jnp.where(ids == rows_named, 1.0, 0.0).astype(jnp.bfloat16)
    high, low = split(table)
    return dot_rows(chosen, high) + dot_rows(chosen, low)


def cold_kernel(asked_ref, table_ref, out_ref):
    out_ref[...] = pick(asked_ref[...], table_ref[...])


def cold_look_up(asked, table):
    count, width = asked.shape[1], table.shape[1]
    return pl.pallas_call(
        cold_kernel,
        out_shape=jax.ShapeDtypeStruct((count, width), jnp.float32),
        compiler_params=pltpu.CompilerParams(vmem_limit_bytes=VMEM_LIMIT),
        cost_estimate=pl.CostEstimate(
            flops=4 * count * table.size, bytes_accessed=4 * table.size, transcendentals=0
        ),
        name="cold_look_up",
    )(asked, table)


def hot_kernel(half, device_ref, asked_ref, own_ref, far_ref, *out_refs):
    slots = asked_ref.shape[1] // 2
    rows = own_ref.shape[0]
    at = device_ref[1] % half
    table = jnp.concatenate([own_ref[...], far_ref[...]], axis=0)
    high, low = split(table)
    lanes = lax.broadcasted_iota(jnp.int32, (1, 2 * slots), 1)
    ids = lax.broadcasted_iota(jnp.int32, (2 * rows, 2 * slots), 0)
    for away in range(half):
        asked = asked_ref[pl.ds(at ^ away, 1), :]
        asked = jnp.where((lanes >= slots) & (asked >= 0), asked + rows, asked)
        chosen = jnp.where(ids == asked, 1.0, 0.0).astype(jnp.bfloat16)
        out_refs[away][...] = dot_rows(chosen, high) + dot_rows(chosen, low)


def hot_look_up(half, device, asked, own, far):
    slots, width = asked.shape[1], own.shape[1]
    vmem = pl.BlockSpec(memory_space=pltpu.VMEM)
    return pl.pallas_call(
        functools.partial(hot_kernel, half),
        in_specs=[pl.BlockSpec(memory_space=pltpu.SMEM)] + [vmem] * 3,
        out_specs=[vmem] * half,
        out_shape=[jax.ShapeDtypeStruct((slots, width), jnp.float32)] * half,
        compiler_params=pltpu.CompilerParams(vmem_limit_bytes=VMEM_LIMIT),
        cost_estimate=pl.CostEstimate(
            flops=8 * half * slots * own.size, bytes_accessed=12 * own.size, transcendentals=0
        ),
        name="hot_look_up",
    )(device, asked, own, far)


def layer_kernel(
    chunks, half, far_mask, device_ref, counts_ref, cold_ref, w_self_ref, w_neigh_ref, cot_ref, *rest
):
    hot_refs = rest[:half]
    src, prod, back = rest[-3:]
    grad_refs = rest[-3 - 2 * chunks : -3]
    hidden_ref = rest[-4 - 2 * chunks]
    n_src = src.shape[1]
    n_hot = n_src - cold_ref.shape[0]
    slots = hot_refs[0].shape[0] // 2
    step = pl.program_id(0)

    @pl.when(step == 0)
    def _():
        for away in range(half):
            owner = device_ref[1] ^ away
            high, low = split(hot_refs[away][...])
            for peer, first in ((owner, 0), (owner ^ far_mask, slots)):
                rows = pl.ds(pl.multiple_of(peer * slots, slots), slots)
                src[0, rows, :] = high[first : first + slots, :]
                src[1, rows, :] = low[first : first + slots, :]
        src[0, n_hot:, :], src[1, n_hot:, :] = split(cold_ref[...])
        prod[:n_src, :] = dot(src[0], w_self_ref[...]).astype(jnp.bfloat16)
        both = dot(src[0], w_neigh_ref[...]) + dot(src[1], w_neigh_ref[...])
        prod[n_src:, :] = (both * (1.0 / FAN)).astype(jnp.bfloat16)
        back[...] = jnp.zeros_like(back)

    pre_act = dot_rows(counts_ref[...], prod[...])
    sigma = 0.5 * jnp.tanh(0.5 * pre_act) + 0.5
    hidden_ref[...] = (pre_act * sigma).astype(jnp.bfloat16)
    slope = sigma * (1.0 + pre_act * (1.0 - sigma))
    masked = (cot_ref[...].astype(jnp.float32) * slope).astype(jnp.bfloat16)
    back[...] += dot(counts_ref[...], masked)

    @pl.when(step == pl.num_programs(0) - 1)
    def _():
        cols = back.shape[1] // chunks

        def self_term(part):
            high, low = split(back[:n_src, pl.ds(part * cols, cols)])
            return dot_rows(src[0], high) + dot_rows(src[0], low)

        def neigh_term(part):
            high, low = split(back[n_src:, pl.ds(part * cols, cols)] * (1.0 / FAN))
            return dot_rows(src[0], high) + dot_rows(src[0], low) + dot_rows(src[1], high)

        @pl.when(device_ref[0] == 0)
        def _():
            for part in range(chunks):
                grad_refs[2 * part][...] = self_term(part)
                grad_refs[2 * part + 1][...] = neigh_term(part)

        @pl.when(device_ref[0] != 0)
        def _():
            for part in range(chunks):
                grad_refs[2 * part][...] = neigh_term(part)
                grad_refs[2 * part + 1][...] = self_term(part)


def layer(call, chunks, far_mask, device, counts, hot_rows, cold_rows, w_self, w_neigh, cotangent, hidden):
    targets, hidden_units = cotangent.shape
    feat_width = w_self.shape[0]
    n_src = counts.shape[0] // 2
    wide = hidden_units // CALLS
    cols = wide // chunks
    block = 512
    whole = lambda i, c: (0, 0)
    column = lambda i, c: (0, call)
    tile = lambda i, c: (i, call)
    in_specs = [
        pl.BlockSpec((2 * n_src, block), lambda i, c: (0, i)),
        pl.BlockSpec(cold_rows.shape, whole),
        pl.BlockSpec((feat_width, wide), column),
        pl.BlockSpec((feat_width, wide), column),
        pl.BlockSpec((block, wide), tile),
    ] + [pl.BlockSpec(rows.shape, whole) for rows in hot_rows]
    operands = [device, counts, cold_rows, w_self, w_neigh, cotangent, *hot_rows]
    aliases = {}
    if hidden is not None:
        in_specs.append(pl.BlockSpec(memory_space=pl.ANY))
        operands.append(hidden)
        aliases = {len(operands) - 1: 0}
    return pl.pallas_call(
        functools.partial(layer_kernel, chunks, len(hot_rows), far_mask),
        grid_spec=pltpu.PrefetchScalarGridSpec(
            num_scalar_prefetch=1,
            grid=(targets // block,),
            in_specs=in_specs,
            out_specs=[pl.BlockSpec((block, wide), tile)]
            + [pl.BlockSpec((feat_width, cols), whole)] * (2 * chunks),
            scratch_shapes=[
                pltpu.VMEM((2, n_src, feat_width), jnp.bfloat16),
                pltpu.VMEM((2 * n_src, wide), jnp.bfloat16),
                pltpu.VMEM((2 * n_src, wide), jnp.float32),
            ],
        ),
        out_shape=[jax.ShapeDtypeStruct((targets, hidden_units), jnp.bfloat16)]
        + [jax.ShapeDtypeStruct((feat_width, cols), jnp.float32)] * (2 * chunks),
        input_output_aliases=aliases,
        compiler_params=pltpu.CompilerParams(vmem_limit_bytes=VMEM_LIMIT),
        cost_estimate=pl.CostEstimate(
            flops=4 * n_src * wide * (2 * targets + 2 * feat_width),
            bytes_accessed=4 * targets * n_src + 4 * targets * wide,
            transcendentals=targets * wide,
        ),
        name=f"layer_{call}",
    )(*operands)


def place_kernel(where_ref, mine, got, other_mine, other_got, *rest):
    out_self, out_neigh = rest[-2:]
    mine_here = pl.program_id(0) == where_ref[1]
    first_core = where_ref[0] == 0
    for here, own, other in ((mine_here, mine, other_mine), (~mine_here, got, other_got)):

        @pl.when(here & first_core)
        def _(own=own, other=other):
            out_self[...] = own[...]
            out_neigh[...] = other[...]

        @pl.when(here & ~first_core)
        def _(own=own, other=other):
            out_self[...] = other[...]
            out_neigh[...] = own[...]


def place(chunk, where, pieces, outs):
    rows, cols = pieces[0].shape
    shape = jax.ShapeDtypeStruct((2 * rows, CHUNKS * cols), jnp.float32)
    return pl.pallas_call(
        place_kernel,
        grid_spec=pltpu.PrefetchScalarGridSpec(
            num_scalar_prefetch=1,
            grid=(2,),
            in_specs=[pl.BlockSpec((rows, cols), lambda i, w: (0, 0))] * 4
            + [pl.BlockSpec(memory_space=pl.ANY)] * len(outs),
            out_specs=[pl.BlockSpec((rows, cols), lambda i, w: (i, chunk))] * 2,
        ),
        out_shape=[shape, shape],
        input_output_aliases={5: 0, 6: 1} if outs else {},
        compiler_params=pltpu.CompilerParams(vmem_limit_bytes=VMEM_LIMIT),
        cost_estimate=pl.CostEstimate(flops=0, bytes_accessed=32 * rows * cols, transcendentals=0),
        name=f"place_chunk_{chunk}",
    )(where, *pieces, *outs)


class Swap:
    def __init__(self, name, mask, bit):
        self.name, self.mask, self.bit = name, mask, bit
        self.pairs = [(i, i ^ mask) for i in range(lax.axis_size(name))]

    def send(self, value):
        return lax.ppermute(value, self.name, self.pairs)


def swaps(name, stride, size, plain=False):
    index = lax.axis_index(name)
    found = []
    step = 1
    while step < size:
        bit = lax.rem(lax.div(index, jnp.int32(stride * step)), jnp.int32(2))
        if 2 * step < size and not plain:
            bit = bit ^ lax.rem(lax.div(index, jnp.int32(stride * step * 2)), jnp.int32(2))
        found.append(Swap(name, stride * (2 * step - 1), bit))
        step *= 2
    return found


def halve(terms, swap):
    rows = terms[0].shape[0] // 2
    low = functools.reduce(jnp.add, [t[:rows] for t in terms])
    high = functools.reduce(jnp.add, [t[rows:] for t in terms])
    out = jnp.where(swap.bit == 0, high, low)
    return [jnp.where(swap.bit == 0, low, high), swap.send(out)]


def double(value, swap):
    got = swap.send(value)
    first = swap.bit == 0
    return jnp.concatenate([jnp.where(first, value, got), jnp.where(first, got, value)], axis=0)


def axis_swaps(plain=False):
    groups, dev_size = lax.axis_size("grp"), lax.axis_size("dev")
    x_size = groups // CORES
    y_size = x_size if dev_size % x_size == 0 else 1
    return (
        swaps("grp", 1, CORES, plain),
        swaps("grp", CORES, x_size, plain),
        swaps("dev", 1, y_size, plain),
        swaps("dev", y_size, dev_size // y_size, plain),
    )


def fetch_rows(hot_table, cold_table, hot_need, cold_need, device):
    core, along_x, along_y, along_z = axis_swaps(plain=True)
    far = along_z[-1]
    half = lax.axis_size("dev") // 2
    me = lax.axis_index("dev")
    slots = hot_need.shape[1]

    spread = along_x + core
    share = hot_table.shape[0] // lax.axis_size("grp")
    which = functools.reduce(jnp.add, [s.bit * (1 << k) for k, s in enumerate(spread)])
    far_table = far.send(lax.dynamic_slice_in_dim(hot_table, which * share, share, axis=0))
    for swap in spread:
        far_table = double(far_table, swap)

    needs = jnp.concatenate([hot_need.reshape(1, -1), cold_need.reshape(1, -1)], axis=1)
    for swap in along_y + along_z[:-1]:
        needs = double(needs, swap)
    hot_asked = jnp.concatenate(
        [
            lax.dynamic_slice_in_dim(needs, peer * slots, slots, axis=1)
            for peer in (me, me ^ far.mask)
        ],
        axis=1,
    )
    for swap in [far] + core + along_x:
        needs = double(needs, swap)
    first = hot_need.size + (lax.axis_index("grp") * 2 * half + me) * cold_need.shape[1]
    cold_asked = lax.dynamic_slice_in_dim(needs, first, cold_need.shape[1], axis=1)
    cold_rows = lax.all_to_all(
        cold_look_up(cold_asked.reshape(1, -1), cold_table),
        ("grp", "dev"),
        split_axis=0,
        concat_axis=0,
        tiled=True,
    )
    served = hot_look_up(half, device, hot_asked, hot_table, far_table)
    pairs = lambda away: [(i, i ^ away) for i in range(2 * half)]
    hot_rows = [served[0]] + [
        lax.ppermute(served[away], "dev", pairs(away)) for away in range(1, half)
    ]
    return hot_rows, cold_rows, far.mask


def sum_over_devices(terms):
    (core,), along_x, along_y, along_z = axis_swaps()
    near_z, far_z = along_z[:1], along_z[1:]
    orders = [
        along_x + along_y + near_z + far_z,
        along_y + along_x + near_z + far_z,
        near_z + along_x + along_y + far_z,
        along_y + along_x + near_z + far_z,
    ]
    grads = []
    for chunk, (keep, send) in enumerate(terms):
        order = orders[chunk]
        parts = [keep, core.send(send)]
        for swap in order[:-1]:
            parts = halve(parts, swap)
        value = parts[0] + parts[1]
        value = value + order[-1].send(value)
        for swap in order[-2:0:-1]:
            value = double(value, swap)
        got = order[0].send(value)
        where = jnp.stack([core.bit, order[0].bit]).astype(jnp.int32)
        grads = place(chunk, where, [value, got, core.send(value), core.send(got)], grads)
    return grads


def body(
    hot_table, cold_table, hot_need, cold_need, self_index, neighbors, w_self, w_neigh, cotangent
):
    n_src = hot_need.size + cold_need.size
    counts = count_matrices(neighbors, self_index, n_src)
    device = jnp.stack([lax.rem(lax.axis_index("grp"), jnp.int32(CORES)), lax.axis_index("dev")])
    hot_rows, cold_rows, far_mask = fetch_rows(hot_table, cold_table, hot_need, cold_need, device)
    hidden = None
    terms = []
    for call in range(CALLS):
        hidden, *grads = layer(
            call,
            CHUNKS // CALLS,
            far_mask,
            device,
            counts,
            hot_rows,
            cold_rows,
            w_self,
            w_neigh,
            cotangent,
            hidden,
        )
        terms += list(zip(grads[::2], grads[1::2]))
    grad_self, grad_neigh = sum_over_devices(terms)
    return (hidden, grad_self, grad_neigh)


def solution(mesh):
    in_specs = (
        P("dev", None),
        P(("grp", "dev"), None),
        P(("grp", "dev"), None),
        P(("grp", "dev"), None),
        P(("grp", "dev")),
        P(("grp", "dev"), None),
        P(),
        P(),
        P(("grp", "dev"), None),
    )
    out_specs = (P(("grp", "dev"), None), P(), P())
    return jax.shard_map(body, mesh=mesh, in_specs=in_specs, out_specs=out_specs, check_vma=False)
```

```python
import functools

import jax
import jax.numpy as jnp
from jax import lax
from jax.experimental import pallas as pl
from jax.experimental.pallas import tpu as pltpu
from jax.sharding import PartitionSpec as P

FAN = 25
CORES = 2
CHUNKS = 4
CALLS = 1
MIB = 1024 * 1024


def split(value):
    high = value.astype(jnp.bfloat16)
    return high, (value - high.astype(jnp.float32)).astype(jnp.bfloat16)


def dot(left, right):
    return jnp.dot(left, right, preferred_element_type=jnp.float32)


def dot_rows(left, right):
    return lax.dot_general(
        left, right, (((0,), (0,)), ((), ())), preferred_element_type=jnp.float32
    )


def count_kernel(slots_ref, self_ref, counts_ref):
    n_src, targets = counts_ref.shape[0] // 2, counts_ref.shape[1]
    step = 32
    slots = slots_ref[...].astype(jnp.int16)
    own = self_ref[...].astype(jnp.int16)

    @pl.loop(0, n_src // step)
    def _(i):
        base = pl.multiple_of(i * step, step)
        ids = (lax.broadcasted_iota(jnp.int32, (step, targets), 0) + base).astype(jnp.int16)
        one = jnp.ones((step, targets), jnp.bfloat16)
        zero = jnp.zeros((step, targets), jnp.bfloat16)
        total = zero
        for j in range(FAN):
            total += jnp.where(slots[j : j + 1, :] == ids, one, zero)
        counts_ref[pl.ds(n_src + base, step), :] = total
        counts_ref[pl.ds(base, step), :] = jnp.where(own == ids, one, zero)


def count_matrices(neighbors, self_index, n_src):
    targets = neighbors.shape[0]
    block = 512
    return pl.pallas_call(
        count_kernel,
        grid=(targets // block,),
        in_specs=[
            pl.BlockSpec((FAN, block), lambda i: (0, i)),
            pl.BlockSpec((1, block), lambda i: (0, i)),
        ],
        out_specs=pl.BlockSpec((2 * n_src, block), lambda i: (0, i)),
        out_shape=jax.ShapeDtypeStruct((2 * n_src, targets), jnp.bfloat16),
        compiler_params=pltpu.CompilerParams(vmem_limit_bytes=60 * MIB),
        cost_estimate=pl.CostEstimate(
            flops=2 * targets * n_src * FAN, bytes_accessed=4 * targets * n_src, transcendentals=0
        ),
        name="count_matrices",
    )(neighbors.T, self_index[None, :])


def pick(rows_named, table):
    ids = lax.broadcasted_iota(jnp.int32, (table.shape[0], rows_named.shape[1]), 0)
    chosen = jnp.where(ids == rows_named, 1.0, 0.0).astype(jnp.bfloat16)
    high, low = split(table)
    return dot_rows(chosen, high) + dot_rows(chosen, low)


def cold_kernel(asked_ref, table_ref, out_ref):
    out_ref[...] = pick(asked_ref[...], table_ref[...])


def cold_look_up(asked, table):
    count, width = asked.shape[1], table.shape[1]
    return pl.pallas_call(
        cold_kernel,
        out_shape=jax.ShapeDtypeStruct((count, width), jnp.float32),
        compiler_params=pltpu.CompilerParams(vmem_limit_bytes=60 * MIB),
        cost_estimate=pl.CostEstimate(
            flops=4 * count * table.size, bytes_accessed=4 * table.size, transcendentals=0
        ),
        name="cold_look_up",
    )(asked, table)


def hot_kernel(half, device_ref, asked_ref, own_ref, far_ref, *out_refs):
    slots = asked_ref.shape[1] // 2
    rows = own_ref.shape[0]
    at = device_ref[1] % half
    table = jnp.concatenate([own_ref[...], far_ref[...]], axis=0)
    high, low = split(table)
    lanes = lax.broadcasted_iota(jnp.int32, (1, 2 * slots), 1)
    ids = lax.broadcasted_iota(jnp.int32, (2 * rows, 2 * slots), 0)
    for away in range(half):
        asked = asked_ref[pl.ds(at ^ away, 1), :]
        asked = jnp.where((lanes >= slots) & (asked >= 0), asked + rows, asked)
        chosen = jnp.where(ids == asked, 1.0, 0.0).astype(jnp.bfloat16)
        out_refs[away][...] = dot_rows(chosen, high) + dot_rows(chosen, low)


def hot_look_up(half, device, asked, own, far):
    slots, width = asked.shape[1], own.shape[1]
    vmem = pl.BlockSpec(memory_space=pltpu.VMEM)
    return pl.pallas_call(
        functools.partial(hot_kernel, half),
        in_specs=[pl.BlockSpec(memory_space=pltpu.SMEM)] + [vmem] * 3,
        out_specs=[vmem] * half,
        out_shape=[jax.ShapeDtypeStruct((slots, width), jnp.float32)] * half,
        compiler_params=pltpu.CompilerParams(vmem_limit_bytes=60 * MIB),
        cost_estimate=pl.CostEstimate(
            flops=8 * half * slots * own.size, bytes_accessed=12 * own.size, transcendentals=0
        ),
        name="hot_look_up",
    )(device, asked, own, far)


def layer_kernel(
    chunks, half, far_mask, device_ref, counts_ref, cold_ref, w_self_ref, w_neigh_ref, cot_ref, *rest
):
    hot_refs = rest[:half]
    src, prod, back = rest[-3:]
    grad_refs = rest[-3 - 2 * chunks : -3]
    hidden_ref = rest[-4 - 2 * chunks]
    n_src = src.shape[1]
    n_hot = n_src - cold_ref.shape[0]
    slots = hot_refs[0].shape[0] // 2
    step = pl.program_id(0)

    @pl.when(step == 0)
    def _():
        for away in range(half):
            owner = device_ref[1] ^ away
            high, low = split(hot_refs[away][...])
            for peer, first in ((owner, 0), (owner ^ far_mask, slots)):
                rows = pl.ds(pl.multiple_of(peer * slots, slots), slots)
                src[0, rows, :] = high[first : first + slots, :]
                src[1, rows, :] = low[first : first + slots, :]
        src[0, n_hot:, :], src[1, n_hot:, :] = split(cold_ref[...])
        prod[:n_src, :] = dot(src[0], w_self_ref[...]).astype(jnp.bfloat16)
        both = dot(src[0], w_neigh_ref[...]) + dot(src[1], w_neigh_ref[...])
        prod[n_src:, :] = (both * (1.0 / FAN)).astype(jnp.bfloat16)
        back[...] = jnp.zeros_like(back)

    pre_act = dot_rows(counts_ref[...], prod[...])
    sigma = 0.5 * jnp.tanh(0.5 * pre_act) + 0.5
    hidden_ref[...] = (pre_act * sigma).astype(jnp.bfloat16)
    slope = sigma * (1.0 + pre_act * (1.0 - sigma))
    masked = (cot_ref[...].astype(jnp.float32) * slope).astype(jnp.bfloat16)
    back[...] += dot(counts_ref[...], masked)

    @pl.when(step == pl.num_programs(0) - 1)
    def _():
        cols = back.shape[1] // chunks

        def self_term(part):
            high, low = split(back[:n_src, pl.ds(part * cols, cols)])
            return dot_rows(src[0], high) + dot_rows(src[0], low)

        def neigh_term(part):
            high, low = split(back[n_src:, pl.ds(part * cols, cols)] * (1.0 / FAN))
            return dot_rows(src[0], high) + dot_rows(src[0], low) + dot_rows(src[1], high)

        @pl.when(device_ref[0] == 0)
        def _():
            for part in range(chunks):
                grad_refs[2 * part][...] = self_term(part)
                grad_refs[2 * part + 1][...] = neigh_term(part)

        @pl.when(device_ref[0] != 0)
        def _():
            for part in range(chunks):
                grad_refs[2 * part][...] = neigh_term(part)
                grad_refs[2 * part + 1][...] = self_term(part)


def layer(call, chunks, far_mask, device, counts, hot_rows, cold_rows, w_self, w_neigh, cotangent, hidden):
    targets, hidden_units = cotangent.shape
    feat_width = w_self.shape[0]
    n_src = counts.shape[0] // 2
    wide = hidden_units // CALLS
    cols = wide // chunks
    block = 512
    whole = lambda i, c: (0, 0)
    column = lambda i, c: (0, call)
    tile = lambda i, c: (i, call)
    in_specs = [
        pl.BlockSpec((2 * n_src, block), lambda i, c: (0, i)),
        pl.BlockSpec(cold_rows.shape, whole),
        pl.BlockSpec((feat_width, wide), column),
        pl.BlockSpec((feat_width, wide), column),
        pl.BlockSpec((block, wide), tile),
    ] + [pl.BlockSpec(rows.shape, whole) for rows in hot_rows]
    operands = [device, counts, cold_rows, w_self, w_neigh, cotangent, *hot_rows]
    aliases = {}
    if hidden is not None:
        aliases = {len(operands): 0}
        in_specs.append(pl.BlockSpec(memory_space=pl.ANY))
        operands.append(hidden)
    return pl.pallas_call(
        functools.partial(layer_kernel, chunks, len(hot_rows), far_mask),
        grid_spec=pltpu.PrefetchScalarGridSpec(
            num_scalar_prefetch=1,
            grid=(targets // block,),
            in_specs=in_specs,
            out_specs=[pl.BlockSpec((block, wide), tile)]
            + [pl.BlockSpec((feat_width, cols), whole)] * (2 * chunks),
            scratch_shapes=[
                pltpu.VMEM((2, n_src, feat_width), jnp.bfloat16),
                pltpu.VMEM((2 * n_src, wide), jnp.bfloat16),
                pltpu.VMEM((2 * n_src, wide), jnp.float32),
            ],
        ),
        out_shape=[jax.ShapeDtypeStruct((targets, hidden_units), jnp.bfloat16)]
        + [jax.ShapeDtypeStruct((feat_width, cols), jnp.float32)] * (2 * chunks),
        input_output_aliases=aliases,
        compiler_params=pltpu.CompilerParams(vmem_limit_bytes=60 * MIB),
        cost_estimate=pl.CostEstimate(
            flops=4 * n_src * wide * (2 * targets + 2 * feat_width),
            bytes_accessed=4 * targets * n_src + 4 * targets * wide,
            transcendentals=targets * wide,
        ),
        name=f"layer_{call}",
    )(*operands)


def place_kernel(where_ref, *rest):
    out_self, out_neigh, sems = rest[-3:]
    pieces = rest[:-3]
    rows, cols = pieces[0].shape

    def put(own, other):
        copies = []
        for chunk in range(len(pieces) // 4):
            first = where_ref[chunk + 1] * rows
            for k, (out, start) in enumerate(
                ((own, first), (own, rows - first), (other, first), (other, rows - first))
            ):
                there = out.at[pl.ds(pl.multiple_of(start, 8), rows), pl.ds(chunk * cols, cols)]
                at = 4 * chunk + k
                copies.append(pltpu.make_async_copy(pieces[at], there, sems.at[at]))
        for copy in copies:
            copy.start()
        for copy in copies:
            copy.wait()

    @pl.when(where_ref[0] == 0)
    def _():
        put(out_self, out_neigh)

    @pl.when(where_ref[0] != 0)
    def _():
        put(out_neigh, out_self)


def place(where, pieces):
    rows, cols = pieces[0].shape
    shape = jax.ShapeDtypeStruct((2 * rows, len(pieces) // 4 * cols), jnp.float32)
    return pl.pallas_call(
        place_kernel,
        in_specs=[pl.BlockSpec(memory_space=pltpu.SMEM)]
        + [pl.BlockSpec(memory_space=pltpu.VMEM)] * len(pieces),
        out_specs=[pl.BlockSpec(memory_space=pl.ANY)] * 2,
        out_shape=[shape, shape],
        scratch_shapes=[pltpu.SemaphoreType.DMA((len(pieces),))],
        compiler_params=pltpu.CompilerParams(vmem_limit_bytes=16 * MIB),
        cost_estimate=pl.CostEstimate(
            flops=0, bytes_accessed=8 * len(pieces) * rows * cols, transcendentals=0
        ),
        name="place",
    )(where, *pieces)


class Swap:
    def __init__(self, name, mask, bit):
        self.name, self.mask, self.bit = name, mask, bit
        self.pairs = [(i, i ^ mask) for i in range(lax.axis_size(name))]

    def send(self, value):
        return lax.ppermute(value, self.name, self.pairs)


def swaps(name, stride, size, plain=False):
    index = lax.axis_index(name)
    found = []
    step = 1
    while step < size:
        bit = lax.rem(lax.div(index, jnp.int32(stride * step)), jnp.int32(2))
        if 2 * step < size and not plain:
            bit = bit ^ lax.rem(lax.div(index, jnp.int32(stride * step * 2)), jnp.int32(2))
        found.append(Swap(name, stride * (2 * step - 1), bit))
        step *= 2
    return found


def cut(terms, swap):
    rows = terms[0].shape[0] // 2
    low = functools.reduce(jnp.add, [t[:rows] for t in terms])
    high = functools.reduce(jnp.add, [t[rows:] for t in terms])
    first = swap.bit == 0
    return jnp.where(first, low, high), jnp.where(first, high, low)


def double(value, swap):
    got = swap.send(value)
    first = swap.bit == 0
    return jnp.concatenate([jnp.where(first, value, got), jnp.where(first, got, value)], axis=0)


def axis_swaps(plain=False):
    groups, dev_size = lax.axis_size("grp"), lax.axis_size("dev")
    x_size = groups // CORES
    y_size = x_size if dev_size % x_size == 0 else 1
    return (
        swaps("grp", 1, CORES, plain),
        swaps("grp", CORES, x_size, plain),
        swaps("dev", 1, y_size, plain),
        swaps("dev", y_size, dev_size // y_size, plain),
    )


def fetch_rows(hot_table, cold_table, hot_need, cold_need, device):
    core, along_x, along_y, along_z = axis_swaps(plain=True)
    far = along_z[-1]
    half = lax.axis_size("dev") // 2
    me = lax.axis_index("dev")
    slots = hot_need.shape[1]

    spread = along_x + core
    share = hot_table.shape[0] // lax.axis_size("grp")
    which = functools.reduce(jnp.add, [s.bit * (1 << k) for k, s in enumerate(spread)])
    far_table = far.send(lax.dynamic_slice_in_dim(hot_table, which * share, share, axis=0))

    both = ("grp", "dev")
    exchange = functools.partial(
        lax.all_to_all, axis_name=both, split_axis=0, concat_axis=0, tiled=True
    )
    devices, cold_slots = cold_need.shape
    hot_list = jnp.broadcast_to(hot_need.reshape(1, -1), (devices, hot_need.size))
    asked = exchange(jnp.concatenate([cold_need, hot_list], axis=1))
    far_table, asked = lax.optimization_barrier((far_table, asked))
    cold_asked = asked[:, :cold_slots]
    first = lax.axis_index("grp") * 2 * half + me - lax.rem(me, jnp.int32(half))
    hot_asked = jnp.concatenate(
        [
            lax.dynamic_slice(asked, (first, cold_slots + peer * slots), (half, slots))
            for peer in (me, me ^ far.mask)
        ],
        axis=1,
    )
    cold_served = cold_look_up(cold_asked.reshape(1, -1), cold_table)
    for swap in spread[:-1]:
        far_table = double(far_table, swap)
    far_table, cold_served = lax.optimization_barrier((far_table, cold_served))
    far_table = double(far_table, spread[-1])
    cold_rows = exchange(cold_served)
    served = hot_look_up(half, device, hot_asked, hot_table, far_table)
    pairs = lambda away: [(i, i ^ away) for i in range(2 * half)]
    hot_rows = [served[0]] + [
        lax.ppermute(served[away], "dev", pairs(away)) for away in range(1, half)
    ]
    return hot_rows, cold_rows, far.mask


def orders_of_sums():
    _, along_x, along_y, along_z = axis_swaps()
    near_z, far_z = along_z[:1], along_z[1:]
    return [
        along_x + along_y + near_z + far_z,
        along_y + along_x + near_z + far_z,
        near_z + along_x + along_y + far_z,
        along_y + along_x + near_z + far_z,
    ]


def sum_chunk(parts, core, order):
    for swap in order[:-1]:
        own, out = cut(parts, swap)
        parts = [own, swap.send(out)]
    value = parts[0] + parts[1]
    value = value + order[-1].send(value)
    for swap in order[-2:0:-1]:
        value = double(value, swap)
    got = order[0].send(value)
    return [value, got, core.send(value), core.send(got)]


def body(
    hot_table, cold_table, hot_need, cold_need, self_index, neighbors, w_self, w_neigh, cotangent
):
    n_src = hot_need.size + cold_need.size
    counts = count_matrices(neighbors, self_index, n_src)
    device = jnp.stack([lax.rem(lax.axis_index("grp"), jnp.int32(CORES)), lax.axis_index("dev")])
    hot_rows, cold_rows, far_mask = fetch_rows(hot_table, cold_table, hot_need, cold_need, device)
    core = axis_swaps()[0][0]
    orders = orders_of_sums()
    chunks = CHUNKS // CALLS
    hidden, sums = None, []
    for call in range(CALLS):
        hidden, *grads = layer(
            call,
            chunks,
            far_mask,
            device,
            counts,
            hot_rows,
            cold_rows,
            w_self,
            w_neigh,
            cotangent,
            hidden,
        )
        for keep, send in zip(grads[::2], grads[1::2]):
            sums.append([keep, core.send(send)])
    pieces = []
    for parts, order in zip(sums, orders):
        pieces += sum_chunk(parts, core, order)
    where = jnp.stack([core.bit] + [order[0].bit for order in orders]).astype(jnp.int32)
    grad_self, grad_neigh = place(where, pieces)
    return (hidden, grad_self, grad_neigh)


def solution(mesh):
    in_specs = (
        P("dev", None),
        P(("grp", "dev"), None),
        P(("grp", "dev"), None),
        P(("grp", "dev"), None),
        P(("grp", "dev")),
        P(("grp", "dev"), None),
        P(),
        P(),
        P(("grp", "dev"), None),
    )
    out_specs = (P(("grp", "dev"), None), P(), P())
    return jax.shard_map(body, mesh=mesh, in_specs=in_specs, out_specs=out_specs, check_vma=False)
```

```python
import functools

import jax
import jax.numpy as jnp
from jax import lax
from jax.experimental import pallas as pl
from jax.experimental.pallas import tpu as pltpu
from jax.sharding import PartitionSpec as P

FAN = 25
CORES = 2
CHUNKS = 4
CALLS = 1
MIB = 1024 * 1024


def split(value):
    high = value.astype(jnp.bfloat16)
    return high, (value - high.astype(jnp.float32)).astype(jnp.bfloat16)


def dot(left, right):
    return jnp.dot(left, right, preferred_element_type=jnp.float32)


def dot_rows(left, right):
    return lax.dot_general(
        left, right, (((0,), (0,)), ((), ())), preferred_element_type=jnp.float32
    )


def count_kernel(slots_ref, self_ref, counts_ref):
    n_src, targets = counts_ref.shape[0] // 2, counts_ref.shape[1]
    step = 32
    slots = slots_ref[...].astype(jnp.int16)
    own = self_ref[...].astype(jnp.int16)

    @pl.loop(0, n_src // step)
    def _(i):
        base = pl.multiple_of(i * step, step)
        ids = (lax.broadcasted_iota(jnp.int32, (step, targets), 0) + base).astype(jnp.int16)
        one = jnp.ones((step, targets), jnp.bfloat16)
        zero = jnp.zeros((step, targets), jnp.bfloat16)
        total = zero
        for j in range(FAN):
            total += jnp.where(slots[j : j + 1, :] == ids, one, zero)
        counts_ref[pl.ds(n_src + base, step), :] = total
        counts_ref[pl.ds(base, step), :] = jnp.where(own == ids, one, zero)


def count_matrices(neighbors, self_index, n_src):
    targets = neighbors.shape[0]
    block = 512
    return pl.pallas_call(
        count_kernel,
        grid=(targets // block,),
        in_specs=[
            pl.BlockSpec((FAN, block), lambda i: (0, i)),
            pl.BlockSpec((1, block), lambda i: (0, i)),
        ],
        out_specs=pl.BlockSpec((2 * n_src, block), lambda i: (0, i)),
        out_shape=jax.ShapeDtypeStruct((2 * n_src, targets), jnp.bfloat16),
        compiler_params=pltpu.CompilerParams(vmem_limit_bytes=60 * MIB),
        cost_estimate=pl.CostEstimate(
            flops=2 * targets * n_src * FAN, bytes_accessed=4 * targets * n_src, transcendentals=0
        ),
        name="count_matrices",
    )(neighbors.T, self_index[None, :])


def pick(rows_named, table):
    ids = lax.broadcasted_iota(jnp.int32, (table.shape[0], rows_named.shape[1]), 0)
    chosen = jnp.where(ids == rows_named, 1.0, 0.0).astype(jnp.bfloat16)
    high, low = split(table)
    return dot_rows(chosen, high) + dot_rows(chosen, low)


def cold_kernel(asked_ref, table_ref, out_ref):
    out_ref[...] = pick(asked_ref[...], table_ref[...])


def cold_look_up(asked, table):
    count, width = asked.shape[1], table.shape[1]
    return pl.pallas_call(
        cold_kernel,
        out_shape=jax.ShapeDtypeStruct((count, width), jnp.float32),
        compiler_params=pltpu.CompilerParams(vmem_limit_bytes=60 * MIB),
        cost_estimate=pl.CostEstimate(
            flops=4 * count * table.size, bytes_accessed=4 * table.size, transcendentals=0
        ),
        name="cold_look_up",
    )(asked, table)


def hot_kernel(half, device_ref, asked_ref, own_ref, far_ref, *out_refs):
    slots = asked_ref.shape[1] // 2
    rows = own_ref.shape[0]
    at = device_ref[1] % half
    table = jnp.concatenate([own_ref[...], far_ref[...]], axis=0)
    high, low = split(table)
    lanes = lax.broadcasted_iota(jnp.int32, (1, 2 * slots), 1)
    ids = lax.broadcasted_iota(jnp.int32, (2 * rows, 2 * slots), 0)
    for away in range(half):
        asked = asked_ref[pl.ds(at ^ away, 1), :]
        asked = jnp.where((lanes >= slots) & (asked >= 0), asked + rows, asked)
        chosen = jnp.where(ids == asked, 1.0, 0.0).astype(jnp.bfloat16)
        out_refs[away][...] = dot_rows(chosen, high) + dot_rows(chosen, low)


def hot_look_up(half, device, asked, own, far):
    slots, width = asked.shape[1], own.shape[1]
    vmem = pl.BlockSpec(memory_space=pltpu.VMEM)
    return pl.pallas_call(
        functools.partial(hot_kernel, half),
        in_specs=[pl.BlockSpec(memory_space=pltpu.SMEM)] + [vmem] * 3,
        out_specs=[vmem] * half,
        out_shape=[jax.ShapeDtypeStruct((slots, width), jnp.float32)] * half,
        compiler_params=pltpu.CompilerParams(vmem_limit_bytes=60 * MIB),
        cost_estimate=pl.CostEstimate(
            flops=8 * half * slots * own.size, bytes_accessed=12 * own.size, transcendentals=0
        ),
        name="hot_look_up",
    )(device, asked, own, far)


def layer_kernel(
    chunks, half, far_mask, device_ref, counts_ref, cold_ref, w_self_ref, w_neigh_ref, cot_ref, *rest
):
    hot_refs = rest[:half]
    src, prod, back = rest[-3:]
    grad_refs = rest[-3 - 2 * chunks : -3]
    hidden_ref = rest[-4 - 2 * chunks]
    n_src = src.shape[1]
    n_hot = n_src - cold_ref.shape[0]
    slots = hot_refs[0].shape[0] // 2
    step = pl.program_id(0)

    @pl.when(step == 0)
    def _():
        for away in range(half):
            owner = device_ref[1] ^ away
            high, low = split(hot_refs[away][...])
            for peer, first in ((owner, 0), (owner ^ far_mask, slots)):
                rows = pl.ds(pl.multiple_of(peer * slots, slots), slots)
                src[0, rows, :] = high[first : first + slots, :]
                src[1, rows, :] = low[first : first + slots, :]
        src[0, n_hot:, :], src[1, n_hot:, :] = split(cold_ref[...])
        prod[:n_src, :] = dot(src[0], w_self_ref[...]).astype(jnp.bfloat16)
        both = dot(src[0], w_neigh_ref[...]) + dot(src[1], w_neigh_ref[...])
        prod[n_src:, :] = (both * (1.0 / FAN)).astype(jnp.bfloat16)
        back[...] = jnp.zeros_like(back)

    pre_act = dot_rows(counts_ref[...], prod[...])
    sigma = 0.5 * jnp.tanh(0.5 * pre_act) + 0.5
    hidden_ref[...] = (pre_act * sigma).astype(jnp.bfloat16)
    slope = sigma * (1.0 + pre_act * (1.0 - sigma))
    masked = (cot_ref[...].astype(jnp.float32) * slope).astype(jnp.bfloat16)
    back[...] += dot(counts_ref[...], masked)

    @pl.when(step == pl.num_programs(0) - 1)
    def _():
        cols = back.shape[1] // chunks

        half_rows = src.shape[2] // 2

        def put(out_ref, part, neigh):
            first = n_src if neigh else 0
            term = back[first : first + n_src, pl.ds(part * cols, cols)]
            high, low = split(term * (1.0 / FAN) if neigh else term)
            bit = device_ref[2 + part]
            for k, at in enumerate((bit, 1 - bit)):
                here = pl.ds(pl.multiple_of(at * half_rows, half_rows), half_rows)
                total = dot_rows(src[0, :, here], high) + dot_rows(src[0, :, here], low)
                if neigh:
                    total += dot_rows(src[1, :, here], high)
                out_ref[k * half_rows : (k + 1) * half_rows, :] = total

        @pl.when(device_ref[0] == 0)
        def _():
            for part in range(chunks):
                put(grad_refs[2 * part], part, False)
                put(grad_refs[2 * part + 1], part, True)

        @pl.when(device_ref[0] != 0)
        def _():
            for part in range(chunks):
                put(grad_refs[2 * part], part, True)
                put(grad_refs[2 * part + 1], part, False)


def layer(call, chunks, far_mask, device, counts, hot_rows, cold_rows, w_self, w_neigh, cotangent, hidden):
    targets, hidden_units = cotangent.shape
    feat_width = w_self.shape[0]
    n_src = counts.shape[0] // 2
    wide = hidden_units // CALLS
    cols = wide // chunks
    block = 512
    whole = lambda i, c: (0, 0)
    column = lambda i, c: (0, call)
    tile = lambda i, c: (i, call)
    in_specs = [
        pl.BlockSpec((2 * n_src, block), lambda i, c: (0, i)),
        pl.BlockSpec(cold_rows.shape, whole),
        pl.BlockSpec((feat_width, wide), column),
        pl.BlockSpec((feat_width, wide), column),
        pl.BlockSpec((block, wide), tile),
    ] + [pl.BlockSpec(rows.shape, whole) for rows in hot_rows]
    operands = [device, counts, cold_rows, w_self, w_neigh, cotangent, *hot_rows]
    aliases = {}
    if hidden is not None:
        aliases = {len(operands): 0}
        in_specs.append(pl.BlockSpec(memory_space=pl.ANY))
        operands.append(hidden)
    return pl.pallas_call(
        functools.partial(layer_kernel, chunks, len(hot_rows), far_mask),
        grid_spec=pltpu.PrefetchScalarGridSpec(
            num_scalar_prefetch=1,
            grid=(targets // block,),
            in_specs=in_specs,
            out_specs=[pl.BlockSpec((block, wide), tile)]
            + [pl.BlockSpec((feat_width, cols), whole)] * (2 * chunks),
            scratch_shapes=[
                pltpu.VMEM((2, n_src, feat_width), jnp.bfloat16),
                pltpu.VMEM((2 * n_src, wide), jnp.bfloat16),
                pltpu.VMEM((2 * n_src, wide), jnp.float32),
            ],
        ),
        out_shape=[jax.ShapeDtypeStruct((targets, hidden_units), jnp.bfloat16)]
        + [jax.ShapeDtypeStruct((feat_width, cols), jnp.float32)] * (2 * chunks),
        input_output_aliases=aliases,
        compiler_params=pltpu.CompilerParams(vmem_limit_bytes=60 * MIB),
        cost_estimate=pl.CostEstimate(
            flops=4 * n_src * wide * (2 * targets + 2 * feat_width),
            bytes_accessed=4 * targets * n_src + 4 * targets * wide,
            transcendentals=targets * wide,
        ),
        name=f"layer_{call}",
    )(*operands)


def place_kernel(where_ref, *rest):
    out_self, out_neigh, sems = rest[-3:]
    pieces = rest[:-3]
    rows, cols = pieces[0].shape

    def put(own, other):
        copies = []
        for chunk in range(len(pieces) // 4):
            first = where_ref[chunk + 1] * rows
            for k, (out, start) in enumerate(
                ((own, first), (own, rows - first), (other, first), (other, rows - first))
            ):
                there = out.at[pl.ds(pl.multiple_of(start, 8), rows), pl.ds(chunk * cols, cols)]
                at = 4 * chunk + k
                copies.append(pltpu.make_async_copy(pieces[at], there, sems.at[at]))
        for copy in copies:
            copy.start()
        for copy in copies:
            copy.wait()

    @pl.when(where_ref[0] == 0)
    def _():
        put(out_self, out_neigh)

    @pl.when(where_ref[0] != 0)
    def _():
        put(out_neigh, out_self)


def place(where, pieces):
    rows, cols = pieces[0].shape
    shape = jax.ShapeDtypeStruct((2 * rows, len(pieces) // 4 * cols), jnp.float32)
    return pl.pallas_call(
        place_kernel,
        in_specs=[pl.BlockSpec(memory_space=pltpu.SMEM)]
        + [pl.BlockSpec(memory_space=pltpu.VMEM)] * len(pieces),
        out_specs=[pl.BlockSpec(memory_space=pl.ANY)] * 2,
        out_shape=[shape, shape],
        scratch_shapes=[pltpu.SemaphoreType.DMA((len(pieces),))],
        compiler_params=pltpu.CompilerParams(vmem_limit_bytes=16 * MIB),
        cost_estimate=pl.CostEstimate(
            flops=0, bytes_accessed=8 * len(pieces) * rows * cols, transcendentals=0
        ),
        name="place",
    )(where, *pieces)


class Swap:
    def __init__(self, name, mask, bit):
        self.name, self.mask, self.bit = name, mask, bit
        self.pairs = [(i, i ^ mask) for i in range(lax.axis_size(name))]

    def send(self, value):
        return lax.ppermute(value, self.name, self.pairs)


def swaps(name, stride, size, plain=False):
    index = lax.axis_index(name)
    found = []
    step = 1
    while step < size:
        bit = lax.rem(lax.div(index, jnp.int32(stride * step)), jnp.int32(2))
        if 2 * step < size and not plain:
            bit = bit ^ lax.rem(lax.div(index, jnp.int32(stride * step * 2)), jnp.int32(2))
        found.append(Swap(name, stride * (2 * step - 1), bit))
        step *= 2
    return found


def cut(terms, swap):
    rows = terms[0].shape[0] // 2
    low = functools.reduce(jnp.add, [t[:rows] for t in terms])
    high = functools.reduce(jnp.add, [t[rows:] for t in terms])
    first = swap.bit == 0
    return jnp.where(first, low, high), jnp.where(first, high, low)


def double(value, swap):
    got = swap.send(value)
    first = swap.bit == 0
    return jnp.concatenate([jnp.where(first, value, got), jnp.where(first, got, value)], axis=0)


def axis_swaps(plain=False):
    groups, dev_size = lax.axis_size("grp"), lax.axis_size("dev")
    x_size = groups // CORES
    y_size = x_size if dev_size % x_size == 0 else 1
    return (
        swaps("grp", 1, CORES, plain),
        swaps("grp", CORES, x_size, plain),
        swaps("dev", 1, y_size, plain),
        swaps("dev", y_size, dev_size // y_size, plain),
    )


def fetch_rows(hot_table, cold_table, hot_need, cold_need, device):
    core, along_x, _, along_z = axis_swaps(plain=True)
    far = along_z[-1]
    half = lax.axis_size("dev") // 2
    me = lax.axis_index("dev")
    slots = hot_need.shape[1]

    spread = along_x + core
    share = hot_table.shape[0] // lax.axis_size("grp")
    which = functools.reduce(jnp.add, [s.bit * (1 << k) for k, s in enumerate(spread)])
    far_table = far.send(lax.dynamic_slice_in_dim(hot_table, which * share, share, axis=0))

    both = ("grp", "dev")
    exchange = functools.partial(
        lax.all_to_all, axis_name=both, split_axis=0, concat_axis=0, tiled=True
    )
    devices, cold_slots = cold_need.shape
    hot_list = jnp.broadcast_to(hot_need.reshape(1, -1), (devices, hot_need.size))
    asked = exchange(jnp.concatenate([cold_need, hot_list], axis=1))
    far_table, asked = lax.optimization_barrier((far_table, asked))
    cold_asked = asked[:, :cold_slots]
    first = lax.axis_index("grp") * 2 * half + me - lax.rem(me, jnp.int32(half))
    hot_asked = jnp.concatenate(
        [
            lax.dynamic_slice(asked, (first, cold_slots + peer * slots), (half, slots))
            for peer in (me, me ^ far.mask)
        ],
        axis=1,
    )
    cold_served = cold_look_up(cold_asked.reshape(1, -1), cold_table)
    for swap in spread[:-1]:
        far_table = double(far_table, swap)
    far_table, cold_served = lax.optimization_barrier((far_table, cold_served))
    far_table = double(far_table, spread[-1])
    cold_rows = exchange(cold_served)
    served = hot_look_up(half, device, hot_asked, hot_table, far_table)
    pairs = lambda away: [(i, i ^ away) for i in range(2 * half)]
    hot_rows = [served[0]] + [
        lax.ppermute(served[away], "dev", pairs(away)) for away in range(1, half)
    ]
    return hot_rows, cold_rows, far.mask


def orders_of_sums():
    _, along_x, along_y, along_z = axis_swaps()
    near_z, far_z = along_z[:1], along_z[1:]
    return [
        along_x + along_y + near_z + far_z,
        along_y + near_z + along_x + far_z,
        near_z + far_z + along_x + along_y,
        along_x + along_y + near_z + far_z,
    ]


def sum_chunk(parts, core, order):
    rows = parts[0].shape[0] // 2
    own, out = (parts[0][k : k + rows] + parts[1][k : k + rows] for k in (0, rows))
    parts = [own, order[0].send(out)]
    for swap in order[1:-1]:
        own, out = cut(parts, swap)
        parts = [own, swap.send(out)]
    value = parts[0] + parts[1]
    value = value + order[-1].send(value)
    for swap in order[-2:0:-1]:
        value = double(value, swap)
    got = order[0].send(value)
    return [value, got, core.send(value), core.send(got)]


def body(
    hot_table, cold_table, hot_need, cold_need, self_index, neighbors, w_self, w_neigh, cotangent
):
    n_src = hot_need.size + cold_need.size
    counts = count_matrices(neighbors, self_index, n_src)
    core = axis_swaps()[0][0]
    orders = orders_of_sums()
    device = jnp.stack([core.bit, lax.axis_index("dev")] + [order[0].bit for order in orders])
    hot_rows, cold_rows, far_mask = fetch_rows(hot_table, cold_table, hot_need, cold_need, device)
    chunks = CHUNKS // CALLS
    hidden, sums = None, []
    for call in range(CALLS):
        hidden, *grads = layer(
            call,
            chunks,
            far_mask,
            device,
            counts,
            hot_rows,
            cold_rows,
            w_self,
            w_neigh,
            cotangent,
            hidden,
        )
        for keep, send in zip(grads[::2], grads[1::2]):
            sums.append([keep, core.send(send)])
    pieces = []
    for parts, order in zip(sums, orders):
        pieces += sum_chunk(parts, core, order)
    where = jnp.stack([core.bit] + [order[0].bit for order in orders]).astype(jnp.int32)
    grad_self, grad_neigh = place(where, pieces)
    return (hidden, grad_self, grad_neigh)


def solution(mesh):
    in_specs = (
        P("dev", None),
        P(("grp", "dev"), None),
        P(("grp", "dev"), None),
        P(("grp", "dev"), None),
        P(("grp", "dev")),
        P(("grp", "dev"), None),
        P(),
        P(),
        P(("grp", "dev"), None),
    )
    out_specs = (P(("grp", "dev"), None), P(), P())
    return jax.shard_map(body, mesh=mesh, in_specs=in_specs, out_specs=out_specs, check_vma=False)
```

```python
import functools

import jax
import jax.numpy as jnp
from jax import lax
from jax.experimental import pallas as pl
from jax.experimental.pallas import tpu as pltpu
from jax.sharding import PartitionSpec as P

FAN = 25
CORES = 2
CHUNKS = 4
CALLS = 1
MIB = 1024 * 1024


def split(value):
    high = value.astype(jnp.bfloat16)
    return high, (value - high.astype(jnp.float32)).astype(jnp.bfloat16)


def dot(left, right):
    return jnp.dot(left, right, preferred_element_type=jnp.float32)


def dot_rows(left, right):
    return lax.dot_general(
        left, right, (((0,), (0,)), ((), ())), preferred_element_type=jnp.float32
    )


def count_kernel(slots_ref, self_ref, counts_ref):
    n_src, targets = counts_ref.shape[0] // 2, counts_ref.shape[1]
    step = 32
    slots = slots_ref[...].astype(jnp.int16)
    own = self_ref[...].astype(jnp.int16)

    @pl.loop(0, n_src // step)
    def _(i):
        base = pl.multiple_of(i * step, step)
        ids = (lax.broadcasted_iota(jnp.int32, (step, targets), 0) + base).astype(jnp.int16)
        one = jnp.ones((step, targets), jnp.bfloat16)
        zero = jnp.zeros((step, targets), jnp.bfloat16)
        total = zero
        for j in range(FAN):
            total += jnp.where(slots[j : j + 1, :] == ids, one, zero)
        counts_ref[pl.ds(n_src + base, step), :] = total
        counts_ref[pl.ds(base, step), :] = jnp.where(own == ids, one, zero)


def count_matrices(neighbors, self_index, n_src):
    targets = neighbors.shape[0]
    block = 512
    return pl.pallas_call(
        count_kernel,
        grid=(targets // block,),
        in_specs=[
            pl.BlockSpec((FAN, block), lambda i: (0, i)),
            pl.BlockSpec((1, block), lambda i: (0, i)),
        ],
        out_specs=pl.BlockSpec((2 * n_src, block), lambda i: (0, i)),
        out_shape=jax.ShapeDtypeStruct((2 * n_src, targets), jnp.bfloat16),
        compiler_params=pltpu.CompilerParams(vmem_limit_bytes=60 * MIB),
        cost_estimate=pl.CostEstimate(
            flops=2 * targets * n_src * FAN, bytes_accessed=4 * targets * n_src, transcendentals=0
        ),
        name="count_matrices",
    )(neighbors.T, self_index[None, :])


def pick(rows_named, table):
    ids = lax.broadcasted_iota(jnp.int32, (table.shape[0], rows_named.shape[1]), 0)
    chosen = jnp.where(ids == rows_named, 1.0, 0.0).astype(jnp.bfloat16)
    high, low = split(table)
    return dot_rows(chosen, high) + dot_rows(chosen, low)


def cold_kernel(asked_ref, table_ref, out_ref):
    devices, slots = out_ref.shape[:2]
    found = pick(asked_ref[...], table_ref[...])
    for device in range(devices):
        out_ref[device] = found[device * slots : (device + 1) * slots, :]


def cold_look_up(asked, table):
    count, width = asked.size, table.shape[1]
    return pl.pallas_call(
        cold_kernel,
        out_shape=jax.ShapeDtypeStruct(asked.shape + (width,), jnp.float32),
        compiler_params=pltpu.CompilerParams(vmem_limit_bytes=60 * MIB),
        cost_estimate=pl.CostEstimate(
            flops=4 * count * table.size, bytes_accessed=4 * table.size, transcendentals=0
        ),
        name="cold_look_up",
    )(asked.reshape(1, -1), table)


def hot_kernel(half, device_ref, asked_ref, own_ref, mine_ref, got_ref, *rest):
    *out_refs, high, low = rest
    slots = asked_ref.shape[1] // 2
    rows = own_ref.shape[0]
    at = device_ref[1] % half
    share = rows // 2
    first = device_ref[0] * share
    for part, start in ((own_ref, 0), (mine_ref, rows + first), (got_ref, 2 * rows - share - first)):
        here = pl.ds(pl.multiple_of(start, share), part.shape[0])
        high[here, :], low[here, :] = split(part[...])
    lanes = lax.broadcasted_iota(jnp.int32, (1, 2 * slots), 1)
    ids = lax.broadcasted_iota(jnp.int32, (2 * rows, 2 * slots), 0)
    for away in range(half):
        asked = asked_ref[pl.ds(at ^ away, 1), :]
        asked = jnp.where((lanes >= slots) & (asked >= 0), asked + rows, asked)
        chosen = jnp.where(ids == asked, 1.0, 0.0).astype(jnp.bfloat16)
        out_refs[away][...] = dot_rows(chosen, high[...]) + dot_rows(chosen, low[...])


def hot_look_up(half, device, asked, own, mine, got):
    slots, width = asked.shape[1], own.shape[1]
    vmem = pl.BlockSpec(memory_space=pltpu.VMEM)
    return pl.pallas_call(
        functools.partial(hot_kernel, half),
        in_specs=[pl.BlockSpec(memory_space=pltpu.SMEM)] + [vmem] * 4,
        out_specs=[vmem] * half,
        out_shape=[jax.ShapeDtypeStruct((slots, width), jnp.float32)] * half,
        scratch_shapes=[pltpu.VMEM((2 * own.shape[0], width), jnp.bfloat16)] * 2,
        compiler_params=pltpu.CompilerParams(vmem_limit_bytes=60 * MIB),
        cost_estimate=pl.CostEstimate(
            flops=8 * half * slots * own.size, bytes_accessed=12 * own.size, transcendentals=0
        ),
        name="hot_look_up",
    )(device, asked, own, mine, got)


def layer_kernel(
    chunks, half, far_mask, device_ref, counts_ref, cold_ref, w_self_ref, w_neigh_ref, cot_ref, *rest
):
    hot_refs = rest[:half]
    src, cold, prod, back, grads, sems = rest[-6:]
    grad_refs = rest[-6 - 2 * chunks : -6]
    hidden_ref = rest[-7 - 2 * chunks]
    n_src = src.shape[1]
    n_hot = n_src - cold.shape[0]
    slots = hot_refs[0].shape[0] // 2
    step = pl.program_id(0)

    @pl.when(step == 0)
    def _():
        for away in range(half):
            owner = device_ref[1] ^ away
            high, low = split(hot_refs[away][...])
            for peer, first in ((owner, 0), (owner ^ far_mask, slots)):
                rows = pl.ds(pl.multiple_of(peer * slots, slots), slots)
                src[0, rows, :] = high[first : first + slots, :]
                src[1, rows, :] = low[first : first + slots, :]
        cold_slots = cold_ref.shape[1]
        for peer in range(cold_ref.shape[0]):
            cold[peer * cold_slots : (peer + 1) * cold_slots, :] = cold_ref[peer]
        src[0, n_hot:, :], src[1, n_hot:, :] = split(cold[...])
        prod[:n_src, :] = dot(src[0], w_self_ref[...]).astype(jnp.bfloat16)
        both = dot(src[0], w_neigh_ref[...]) + dot(src[1], w_neigh_ref[...])
        prod[n_src:, :] = (both * (1.0 / FAN)).astype(jnp.bfloat16)
        back[...] = jnp.zeros_like(back)

    pre_act = dot_rows(counts_ref[...], prod[...])
    sigma = 0.5 * jnp.tanh(0.5 * pre_act) + 0.5
    hidden_ref[...] = (pre_act * sigma).astype(jnp.bfloat16)
    slope = sigma * (1.0 + pre_act * (1.0 - sigma))
    masked = (cot_ref[...].astype(jnp.float32) * slope).astype(jnp.bfloat16)
    back[...] += dot(counts_ref[...], masked)

    @pl.when(step == pl.num_programs(0) - 1)
    def _():
        cols = back.shape[1] // chunks

        half_rows = src.shape[2] // 2

        def put(at, part, neigh):
            first = n_src if neigh else 0
            term = back[first : first + n_src, pl.ds(part * cols, cols)]
            term = (term * (1.0 / FAN) if neigh else term).astype(jnp.bfloat16)
            bit = device_ref[2 + part]
            for k, half_at in enumerate((bit, 1 - bit)):
                here = pl.ds(pl.multiple_of(half_at * half_rows, half_rows), half_rows)
                total = dot_rows(src[0, :, here], term)
                if neigh:
                    total += dot_rows(src[1, :, here], term)
                grads[at, k * half_rows : (k + 1) * half_rows, :] = total
            pltpu.make_async_copy(grads.at[at], grad_refs[at], sems.at[at]).start()

        @pl.when(device_ref[0] == 0)
        def _():
            for part in range(chunks):
                put(2 * part, part, False)
                put(2 * part + 1, part, True)

        @pl.when(device_ref[0] != 0)
        def _():
            for part in range(chunks):
                put(2 * part, part, True)
                put(2 * part + 1, part, False)

        for at in range(2 * chunks):
            pltpu.make_async_copy(grads.at[at], grad_refs[at], sems.at[at]).wait()


def layer(call, chunks, far_mask, device, counts, hot_rows, cold_rows, w_self, w_neigh, cotangent, hidden):
    targets, hidden_units = cotangent.shape
    feat_width = w_self.shape[0]
    n_src = counts.shape[0] // 2
    wide = hidden_units // CALLS
    cols = wide // chunks
    block = 512
    whole = lambda i, c: (0, 0)
    column = lambda i, c: (0, call)
    tile = lambda i, c: (i, call)
    in_specs = [
        pl.BlockSpec((2 * n_src, block), lambda i, c: (0, i)),
        pl.BlockSpec(cold_rows.shape, lambda i, c: (0, 0, 0)),
        pl.BlockSpec((feat_width, wide), column),
        pl.BlockSpec((feat_width, wide), column),
        pl.BlockSpec((block, wide), tile),
    ] + [pl.BlockSpec(rows.shape, whole) for rows in hot_rows]
    operands = [device, counts, cold_rows, w_self, w_neigh, cotangent, *hot_rows]
    aliases = {}
    if hidden is not None:
        aliases = {len(operands): 0}
        in_specs.append(pl.BlockSpec(memory_space=pl.ANY))
        operands.append(hidden)
    return pl.pallas_call(
        functools.partial(layer_kernel, chunks, len(hot_rows), far_mask),
        grid_spec=pltpu.PrefetchScalarGridSpec(
            num_scalar_prefetch=1,
            grid=(targets // block,),
            in_specs=in_specs,
            out_specs=[pl.BlockSpec((block, wide), tile)]
            + [pl.BlockSpec(memory_space=pl.ANY)] * (2 * chunks),
            scratch_shapes=[
                pltpu.VMEM((2, n_src, feat_width), jnp.bfloat16),
                pltpu.VMEM((cold_rows.shape[0] * cold_rows.shape[1], feat_width), jnp.float32),
                pltpu.VMEM((2 * n_src, wide), jnp.bfloat16),
                pltpu.VMEM((2 * n_src, wide), jnp.float32),
                pltpu.VMEM((2 * chunks, feat_width, cols), jnp.float32),
                pltpu.SemaphoreType.DMA((2 * chunks,)),
            ],
        ),
        out_shape=[jax.ShapeDtypeStruct((targets, hidden_units), jnp.bfloat16)]
        + [jax.ShapeDtypeStruct((feat_width, cols), jnp.float32)] * (2 * chunks),
        input_output_aliases=aliases,
        compiler_params=pltpu.CompilerParams(vmem_limit_bytes=60 * MIB),
        cost_estimate=pl.CostEstimate(
            flops=4 * n_src * wide * (2 * targets + 2 * feat_width),
            bytes_accessed=4 * targets * n_src + 4 * targets * wide,
            transcendentals=targets * wide,
        ),
        name=f"layer_{call}",
    )(*operands)


def place_kernel(where_ref, *rest):
    out_self, out_neigh, sems = rest[-3:]
    pieces = rest[:-3]
    rows, cols = pieces[0].shape

    def put(own, other):
        copies = []
        for chunk in range(len(pieces) // 4):
            first = where_ref[chunk + 1] * rows
            for k, (out, start) in enumerate(
                ((own, first), (own, rows - first), (other, first), (other, rows - first))
            ):
                there = out.at[pl.ds(pl.multiple_of(start, 8), rows), pl.ds(chunk * cols, cols)]
                at = 4 * chunk + k
                copies.append(pltpu.make_async_copy(pieces[at], there, sems.at[at]))
        for copy in copies:
            copy.start()
        for copy in copies:
            copy.wait()

    @pl.when(where_ref[0] == 0)
    def _():
        put(out_self, out_neigh)

    @pl.when(where_ref[0] != 0)
    def _():
        put(out_neigh, out_self)


def place(where, pieces):
    rows, cols = pieces[0].shape
    shape = jax.ShapeDtypeStruct((2 * rows, len(pieces) // 4 * cols), jnp.float32)
    return pl.pallas_call(
        place_kernel,
        in_specs=[pl.BlockSpec(memory_space=pltpu.SMEM)]
        + [pl.BlockSpec(memory_space=pltpu.VMEM)] * len(pieces),
        out_specs=[pl.BlockSpec(memory_space=pl.ANY)] * 2,
        out_shape=[shape, shape],
        scratch_shapes=[pltpu.SemaphoreType.DMA((len(pieces),))],
        compiler_params=pltpu.CompilerParams(vmem_limit_bytes=16 * MIB),
        cost_estimate=pl.CostEstimate(
            flops=0, bytes_accessed=8 * len(pieces) * rows * cols, transcendentals=0
        ),
        name="place",
    )(where, *pieces)


class Swap:
    def __init__(self, name, mask, bit):
        self.name, self.mask, self.bit = name, mask, bit
        self.pairs = [(i, i ^ mask) for i in range(lax.axis_size(name))]

    def send(self, value):
        return lax.ppermute(value, self.name, self.pairs)


def swaps(name, stride, size, plain=False):
    index = lax.axis_index(name)
    found = []
    step = 1
    while step < size:
        bit = lax.rem(lax.div(index, jnp.int32(stride * step)), jnp.int32(2))
        if 2 * step < size and not plain:
            bit = bit ^ lax.rem(lax.div(index, jnp.int32(stride * step * 2)), jnp.int32(2))
        found.append(Swap(name, stride * (2 * step - 1), bit))
        step *= 2
    return found


def cut(terms, swap):
    rows = terms[0].shape[0] // 2
    low = functools.reduce(jnp.add, [t[:rows] for t in terms])
    high = functools.reduce(jnp.add, [t[rows:] for t in terms])
    first = swap.bit == 0
    return jnp.where(first, low, high), jnp.where(first, high, low)


def double(value, swap):
    got = swap.send(value)
    first = swap.bit == 0
    return jnp.concatenate([jnp.where(first, value, got), jnp.where(first, got, value)], axis=0)


def axis_swaps(plain=False):
    groups, dev_size = lax.axis_size("grp"), lax.axis_size("dev")
    x_size = groups // CORES
    y_size = x_size if dev_size % x_size == 0 else 1
    return (
        swaps("grp", 1, CORES, plain),
        swaps("grp", CORES, x_size, plain),
        swaps("dev", 1, y_size, plain),
        swaps("dev", y_size, dev_size // y_size, plain),
    )


def fetch_rows(hot_table, cold_table, hot_need, cold_need, device):
    core, along_x, _, along_z = axis_swaps(plain=True)
    far = along_z[-1]
    half = lax.axis_size("dev") // 2
    me = lax.axis_index("dev")
    slots = hot_need.shape[1]

    (core,) = core
    spread = along_x + [core]
    share = hot_table.shape[0] // lax.axis_size("grp")
    which = functools.reduce(jnp.add, [s.bit * (1 << k) for k, s in enumerate(spread)])
    far_table = far.send(lax.dynamic_slice_in_dim(hot_table, which * share, share, axis=0))

    both = ("grp", "dev")
    exchange = functools.partial(
        lax.all_to_all, axis_name=both, split_axis=0, concat_axis=0, tiled=True
    )
    devices, cold_slots = cold_need.shape
    hot_list = jnp.broadcast_to(hot_need.reshape(1, -1), (devices, hot_need.size))
    asked = exchange(jnp.concatenate([cold_need, hot_list], axis=1))
    far_table, asked = lax.optimization_barrier((far_table, asked))
    cold_asked = asked[:, :cold_slots]
    first = lax.axis_index("grp") * 2 * half + me - lax.rem(me, jnp.int32(half))
    hot_asked = jnp.concatenate(
        [
            lax.dynamic_slice(asked, (first, cold_slots + peer * slots), (half, slots))
            for peer in (me, me ^ far.mask)
        ],
        axis=1,
    )
    cold_served = cold_look_up(cold_asked, cold_table)
    for swap in along_x:
        far_table = double(far_table, swap)
    far_table, cold_served = lax.optimization_barrier((far_table, cold_served))
    cold_rows = exchange(cold_served)
    served = hot_look_up(half, device, hot_asked, hot_table, far_table, core.send(far_table))
    pairs = lambda away: [(i, i ^ away) for i in range(2 * half)]
    hot_rows = [served[0]] + [
        lax.ppermute(served[away], "dev", pairs(away)) for away in range(1, half)
    ]
    return hot_rows, cold_rows, far.mask


def orders_of_sums():
    _, along_x, along_y, along_z = axis_swaps()
    near_z, far_z = along_z[:1], along_z[1:]
    return [
        along_x + along_y + near_z + far_z,
        along_y + near_z + along_x + far_z,
        near_z + far_z + along_x + along_y,
        along_x + along_y + near_z + far_z,
    ]


def sum_chunk(parts, core, order):
    rows = parts[0].shape[0] // 2
    own, out = (parts[0][k : k + rows] + parts[1][k : k + rows] for k in (0, rows))
    parts = [own, order[0].send(out)]
    for swap in order[1:-1]:
        own, out = cut(parts, swap)
        parts = [own, swap.send(out)]
    value = parts[0] + parts[1]
    value = value + order[-1].send(value)
    for swap in order[-2:0:-1]:
        value = double(value, swap)
    got = order[0].send(value)
    return [value, got, core.send(value), core.send(got)]


def body(
    hot_table, cold_table, hot_need, cold_need, self_index, neighbors, w_self, w_neigh, cotangent
):
    n_src = hot_need.size + cold_need.size
    counts = count_matrices(neighbors, self_index, n_src)
    core = axis_swaps()[0][0]
    orders = orders_of_sums()
    device = jnp.stack([core.bit, lax.axis_index("dev")] + [order[0].bit for order in orders])
    hot_rows, cold_rows, far_mask = fetch_rows(hot_table, cold_table, hot_need, cold_need, device)
    chunks = CHUNKS // CALLS
    hidden, sums = None, []
    for call in range(CALLS):
        hidden, *grads = layer(
            call,
            chunks,
            far_mask,
            device,
            counts,
            hot_rows,
            cold_rows,
            w_self,
            w_neigh,
            cotangent,
            hidden,
        )
        for keep, send in zip(grads[::2], grads[1::2]):
            sums.append([keep, core.send(send)])
    pieces = []
    for parts, order in zip(sums, orders):
        pieces += sum_chunk(parts, core, order)
    where = jnp.stack([core.bit] + [order[0].bit for order in orders]).astype(jnp.int32)
    grad_self, grad_neigh = place(where, pieces)
    return (hidden, grad_self, grad_neigh)


def solution(mesh):
    in_specs = (
        P("dev", None),
        P(("grp", "dev"), None),
        P(("grp", "dev"), None),
        P(("grp", "dev"), None),
        P(("grp", "dev")),
        P(("grp", "dev"), None),
        P(),
        P(),
        P(("grp", "dev"), None),
    )
    out_specs = (P(("grp", "dev"), None), P(), P())
    return jax.shard_map(body, mesh=mesh, in_specs=in_specs, out_specs=out_specs, check_vma=False)
```

```python
import functools

import jax
import jax.numpy as jnp
from jax import lax
from jax.experimental import pallas as pl
from jax.experimental.pallas import tpu as pltpu
from jax.sharding import PartitionSpec as P

FAN = 25
CORES = 2
CHUNKS = 4
CALLS = 1
MIB = 1024 * 1024


def split(value):
    high = value.astype(jnp.bfloat16)
    return high, (value - high.astype(jnp.float32)).astype(jnp.bfloat16)


def dot(left, right):
    return jnp.dot(left, right, preferred_element_type=jnp.float32)


def dot_rows(left, right):
    return lax.dot_general(
        left, right, (((0,), (0,)), ((), ())), preferred_element_type=jnp.float32
    )


def count_kernel(slots_ref, self_ref, counts_ref):
    n_src, targets = counts_ref.shape[0] // 2, counts_ref.shape[1]
    step = 32
    slots = slots_ref[...].astype(jnp.int16)
    own = self_ref[...].astype(jnp.int16)

    @pl.loop(0, n_src // step)
    def _(i):
        base = pl.multiple_of(i * step, step)
        ids = (lax.broadcasted_iota(jnp.int32, (step, targets), 0) + base).astype(jnp.int16)
        one = jnp.ones((step, targets), jnp.bfloat16)
        zero = jnp.zeros((step, targets), jnp.bfloat16)
        total = zero
        for j in range(FAN):
            total += jnp.where(slots[j : j + 1, :] == ids, one, zero)
        counts_ref[pl.ds(n_src + base, step), :] = total
        counts_ref[pl.ds(base, step), :] = jnp.where(own == ids, one, zero)


def count_matrices(neighbors, self_index, n_src):
    targets = neighbors.shape[0]
    block = 512
    return pl.pallas_call(
        count_kernel,
        grid=(targets // block,),
        in_specs=[
            pl.BlockSpec((FAN, block), lambda i: (0, i)),
            pl.BlockSpec((1, block), lambda i: (0, i)),
        ],
        out_specs=pl.BlockSpec((2 * n_src, block), lambda i: (0, i)),
        out_shape=jax.ShapeDtypeStruct((2 * n_src, targets), jnp.bfloat16),
        compiler_params=pltpu.CompilerParams(vmem_limit_bytes=60 * MIB),
        cost_estimate=pl.CostEstimate(
            flops=2 * targets * n_src * FAN, bytes_accessed=4 * targets * n_src, transcendentals=0
        ),
        name="count_matrices",
    )(neighbors.T, self_index[None, :])


def pick(rows_named, table):
    ids = lax.broadcasted_iota(jnp.int32, (table.shape[0], rows_named.shape[1]), 0)
    chosen = jnp.where(ids == rows_named, 1.0, 0.0).astype(jnp.bfloat16)
    high, low = split(table)
    return dot_rows(chosen, high) + dot_rows(chosen, low)


def cold_kernel(asked_ref, table_ref, out_ref):
    devices, slots = out_ref.shape[:2]
    found = pick(asked_ref[...], table_ref[...])
    for device in range(devices):
        out_ref[device] = found[device * slots : (device + 1) * slots, :]


def cold_look_up(asked, table):
    count, width = asked.size, table.shape[1]
    return pl.pallas_call(
        cold_kernel,
        out_shape=jax.ShapeDtypeStruct(asked.shape + (width,), jnp.float32),
        compiler_params=pltpu.CompilerParams(vmem_limit_bytes=60 * MIB),
        cost_estimate=pl.CostEstimate(
            flops=4 * count * table.size, bytes_accessed=4 * table.size, transcendentals=0
        ),
        name="cold_look_up",
    )(asked.reshape(1, -1), table)


def hot_kernel(half, device_ref, asked_ref, own_ref, mine_ref, got_ref, *rest):
    *out_refs, high, low = rest
    slots = asked_ref.shape[1] // 2
    rows = own_ref.shape[0]
    at = device_ref[1] % half
    share = rows // 2
    first = device_ref[0] * share
    for part, start in ((own_ref, 0), (mine_ref, rows + first), (got_ref, 2 * rows - share - first)):
        here = pl.ds(pl.multiple_of(start, share), part.shape[0])
        high[here, :], low[here, :] = split(part[...])
    lanes = lax.broadcasted_iota(jnp.int32, (1, 2 * slots), 1)
    ids = lax.broadcasted_iota(jnp.int32, (2 * rows, 2 * slots), 0)
    for away in range(half):
        asked = asked_ref[pl.ds(at ^ away, 1), :]
        asked = jnp.where((lanes >= slots) & (asked >= 0), asked + rows, asked)
        chosen = jnp.where(ids == asked, 1.0, 0.0).astype(jnp.bfloat16)
        out_refs[away][...] = dot_rows(chosen, high[...]) + dot_rows(chosen, low[...])


def hot_look_up(half, device, asked, own, mine, got):
    slots, width = asked.shape[1], own.shape[1]
    vmem = pl.BlockSpec(memory_space=pltpu.VMEM)
    return pl.pallas_call(
        functools.partial(hot_kernel, half),
        in_specs=[pl.BlockSpec(memory_space=pltpu.SMEM)] + [vmem] * 4,
        out_specs=[vmem] * half,
        out_shape=[jax.ShapeDtypeStruct((slots, width), jnp.float32)] * half,
        scratch_shapes=[pltpu.VMEM((2 * own.shape[0], width), jnp.bfloat16)] * 2,
        compiler_params=pltpu.CompilerParams(vmem_limit_bytes=24 * MIB),
        cost_estimate=pl.CostEstimate(
            flops=8 * half * slots * own.size, bytes_accessed=12 * own.size, transcendentals=0
        ),
        name="hot_look_up",
    )(device, asked, own, mine, got)


def layer_kernel(
    chunks, half, far_mask, device_ref, counts_ref, cold_ref, w_self_ref, w_neigh_ref, cot_ref, *rest
):
    hot_refs = rest[:half]
    src, cold, prod, back, grads, sems = rest[-6:]
    grad_refs = rest[-6 - 2 * chunks : -6]
    hidden_ref = rest[-7 - 2 * chunks]
    n_src = src.shape[1]
    n_hot = n_src - cold.shape[0]
    slots = hot_refs[0].shape[0] // 2
    step = pl.program_id(0)

    @pl.when(step == 0)
    def _():
        for away in range(half):
            owner = device_ref[1] ^ away
            high, low = split(hot_refs[away][...])
            for peer, first in ((owner, 0), (owner ^ far_mask, slots)):
                rows = pl.ds(pl.multiple_of(peer * slots, slots), slots)
                src[0, rows, :] = high[first : first + slots, :]
                src[1, rows, :] = low[first : first + slots, :]
        cold_slots = cold_ref.shape[1]
        for peer in range(cold_ref.shape[0]):
            cold[peer * cold_slots : (peer + 1) * cold_slots, :] = cold_ref[peer]
        src[0, n_hot:, :], src[1, n_hot:, :] = split(cold[...])
        prod[:n_src, :] = dot(src[0], w_self_ref[...]).astype(jnp.bfloat16)
        both = dot(src[0], w_neigh_ref[...]) + dot(src[1], w_neigh_ref[...])
        prod[n_src:, :] = (both * (1.0 / FAN)).astype(jnp.bfloat16)
        back[...] = jnp.zeros_like(back)

    pre_act = dot_rows(counts_ref[...], prod[...])
    sigma = 0.5 * jnp.tanh(0.5 * pre_act) + 0.5
    hidden_ref[...] = (pre_act * sigma).astype(jnp.bfloat16)
    slope = sigma * (1.0 + pre_act * (1.0 - sigma))
    masked = (cot_ref[...].astype(jnp.float32) * slope).astype(jnp.bfloat16)
    back[...] += dot(counts_ref[...], masked)

    @pl.when(step == pl.num_programs(0) - 1)
    def _():
        cols = back.shape[1] // chunks

        half_rows = src.shape[2] // 2

        def put(at, part, neigh):
            first = n_src if neigh else 0
            term = back[first : first + n_src, pl.ds(part * cols, cols)]
            term = (term * (1.0 / FAN) if neigh else term).astype(jnp.bfloat16)
            bit = device_ref[2 + part]
            for k, half_at in enumerate((bit, 1 - bit)):
                here = pl.ds(pl.multiple_of(half_at * half_rows, half_rows), half_rows)
                total = dot_rows(src[0, :, here], term)
                if neigh:
                    total += dot_rows(src[1, :, here], term)
                grads[at, k * half_rows : (k + 1) * half_rows, :] = total
            pltpu.make_async_copy(grads.at[at], grad_refs[at], sems.at[at]).start()

        @pl.when(device_ref[0] == 0)
        def _():
            for part in range(chunks):
                put(2 * part, part, False)
                put(2 * part + 1, part, True)

        @pl.when(device_ref[0] != 0)
        def _():
            for part in range(chunks):
                put(2 * part, part, True)
                put(2 * part + 1, part, False)

        for at in range(2 * chunks):
            pltpu.make_async_copy(grads.at[at], grad_refs[at], sems.at[at]).wait()


def layer(call, chunks, far_mask, device, counts, hot_rows, cold_rows, w_self, w_neigh, cotangent, hidden):
    targets, hidden_units = cotangent.shape
    feat_width = w_self.shape[0]
    n_src = counts.shape[0] // 2
    wide = hidden_units // CALLS
    cols = wide // chunks
    block = 1024
    whole = lambda i, c: (0, 0)
    column = lambda i, c: (0, call)
    tile = lambda i, c: (i, call)
    in_specs = [
        pl.BlockSpec((2 * n_src, block), lambda i, c: (0, i)),
        pl.BlockSpec(cold_rows.shape, lambda i, c: (0, 0, 0)),
        pl.BlockSpec((feat_width, wide), column),
        pl.BlockSpec((feat_width, wide), column),
        pl.BlockSpec((block, wide), tile),
    ] + [pl.BlockSpec(rows.shape, whole) for rows in hot_rows]
    operands = [device, counts, cold_rows, w_self, w_neigh, cotangent, *hot_rows]
    aliases = {}
    if hidden is not None:
        aliases = {len(operands): 0}
        in_specs.append(pl.BlockSpec(memory_space=pl.ANY))
        operands.append(hidden)
    return pl.pallas_call(
        functools.partial(layer_kernel, chunks, len(hot_rows), far_mask),
        grid_spec=pltpu.PrefetchScalarGridSpec(
            num_scalar_prefetch=1,
            grid=(targets // block,),
            in_specs=in_specs,
            out_specs=[pl.BlockSpec((block, wide), tile)]
            + [pl.BlockSpec(memory_space=pl.ANY)] * (2 * chunks),
            scratch_shapes=[
                pltpu.VMEM((2, n_src, feat_width), jnp.bfloat16),
                pltpu.VMEM((cold_rows.shape[0] * cold_rows.shape[1], feat_width), jnp.float32),
                pltpu.VMEM((2 * n_src, wide), jnp.bfloat16),
                pltpu.VMEM((2 * n_src, wide), jnp.float32),
                pltpu.VMEM((2 * chunks, feat_width, cols), jnp.float32),
                pltpu.SemaphoreType.DMA((2 * chunks,)),
            ],
        ),
        out_shape=[jax.ShapeDtypeStruct((targets, hidden_units), jnp.bfloat16)]
        + [jax.ShapeDtypeStruct((feat_width, cols), jnp.float32)] * (2 * chunks),
        input_output_aliases=aliases,
        compiler_params=pltpu.CompilerParams(vmem_limit_bytes=60 * MIB),
        cost_estimate=pl.CostEstimate(
            flops=4 * n_src * wide * (2 * targets + 2 * feat_width),
            bytes_accessed=4 * targets * n_src + 4 * targets * wide,
            transcendentals=targets * wide,
        ),
        name=f"layer_{call}",
    )(*operands)


def place_kernel(where_ref, *rest):
    out_self, out_neigh, sems = rest[-3:]
    pieces = rest[:-3]
    rows, cols = pieces[0].shape

    def put(own, other):
        copies = []
        for chunk in range(len(pieces) // 4):
            first = where_ref[chunk + 1] * rows
            for k, (out, start) in enumerate(
                ((own, first), (own, rows - first), (other, first), (other, rows - first))
            ):
                there = out.at[pl.ds(pl.multiple_of(start, 8), rows), pl.ds(chunk * cols, cols)]
                at = 4 * chunk + k
                copies.append(pltpu.make_async_copy(pieces[at], there, sems.at[at]))
        for copy in copies:
            copy.start()
        for copy in copies:
            copy.wait()

    @pl.when(where_ref[0] == 0)
    def _():
        put(out_self, out_neigh)

    @pl.when(where_ref[0] != 0)
    def _():
        put(out_neigh, out_self)


def place(where, pieces):
    rows, cols = pieces[0].shape
    shape = jax.ShapeDtypeStruct((2 * rows, len(pieces) // 4 * cols), jnp.float32)
    return pl.pallas_call(
        place_kernel,
        in_specs=[pl.BlockSpec(memory_space=pltpu.SMEM)]
        + [pl.BlockSpec(memory_space=pltpu.VMEM)] * len(pieces),
        out_specs=[pl.BlockSpec(memory_space=pl.ANY)] * 2,
        out_shape=[shape, shape],
        scratch_shapes=[pltpu.SemaphoreType.DMA((len(pieces),))],
        compiler_params=pltpu.CompilerParams(vmem_limit_bytes=8 * MIB),
        cost_estimate=pl.CostEstimate(
            flops=0, bytes_accessed=8 * len(pieces) * rows * cols, transcendentals=0
        ),
        name="place",
    )(where, *pieces)


class Swap:
    def __init__(self, name, mask, bit):
        self.name, self.mask, self.bit = name, mask, bit
        self.pairs = [(i, i ^ mask) for i in range(lax.axis_size(name))]

    def send(self, value):
        return lax.ppermute(value, self.name, self.pairs)


def swaps(name, stride, size, plain=False):
    index = lax.axis_index(name)
    found = []
    step = 1
    while step < size:
        bit = lax.rem(lax.div(index, jnp.int32(stride * step)), jnp.int32(2))
        if 2 * step < size and not plain:
            bit = bit ^ lax.rem(lax.div(index, jnp.int32(stride * step * 2)), jnp.int32(2))
        found.append(Swap(name, stride * (2 * step - 1), bit))
        step *= 2
    return found


def cut(terms, swap):
    rows = terms[0].shape[0] // 2
    low = functools.reduce(jnp.add, [t[:rows] for t in terms])
    high = functools.reduce(jnp.add, [t[rows:] for t in terms])
    first = swap.bit == 0
    return jnp.where(first, low, high), jnp.where(first, high, low)


def double(value, swap):
    got = swap.send(value)
    first = swap.bit == 0
    return jnp.concatenate([jnp.where(first, value, got), jnp.where(first, got, value)], axis=0)


def axis_swaps(plain=False):
    groups, dev_size = lax.axis_size("grp"), lax.axis_size("dev")
    x_size = groups // CORES
    y_size = x_size if dev_size % x_size == 0 else 1
    return (
        swaps("grp", 1, CORES, plain),
        swaps("grp", CORES, x_size, plain),
        swaps("dev", 1, y_size, plain),
        swaps("dev", y_size, dev_size // y_size, plain),
    )


def fetch_rows(hot_table, cold_table, hot_need, cold_need, device):
    core, along_x, _, along_z = axis_swaps(plain=True)
    far = along_z[-1]
    half = lax.axis_size("dev") // 2
    me = lax.axis_index("dev")
    slots = hot_need.shape[1]

    (core,) = core
    spread = along_x + [core]
    share = hot_table.shape[0] // lax.axis_size("grp")
    which = functools.reduce(jnp.add, [s.bit * (1 << k) for k, s in enumerate(spread)])
    far_table = far.send(lax.dynamic_slice_in_dim(hot_table, which * share, share, axis=0))

    both = ("grp", "dev")
    exchange = functools.partial(
        lax.all_to_all, axis_name=both, split_axis=0, concat_axis=0, tiled=True
    )
    devices, cold_slots = cold_need.shape
    hot_list = jnp.broadcast_to(hot_need.reshape(1, -1), (devices, hot_need.size))
    asked = exchange(jnp.concatenate([cold_need, hot_list], axis=1))
    far_table, asked = lax.optimization_barrier((far_table, asked))
    cold_asked = asked[:, :cold_slots]
    first = lax.axis_index("grp") * 2 * half + me - lax.rem(me, jnp.int32(half))
    hot_asked = jnp.concatenate(
        [
            lax.dynamic_slice(asked, (first, cold_slots + peer * slots), (half, slots))
            for peer in (me, me ^ far.mask)
        ],
        axis=1,
    )
    cold_served = cold_look_up(cold_asked, cold_table)
    for swap in along_x:
        far_table = double(far_table, swap)
    far_table, cold_served = lax.optimization_barrier((far_table, cold_served))
    cold_rows = exchange(cold_served)
    served = hot_look_up(half, device, hot_asked, hot_table, far_table, core.send(far_table))
    pairs = lambda away: [(i, i ^ away) for i in range(2 * half)]
    hot_rows = [served[0]] + [
        lax.ppermute(served[away], "dev", pairs(away)) for away in range(1, half)
    ]
    return hot_rows, cold_rows, far.mask


def orders_of_sums():
    _, along_x, along_y, along_z = axis_swaps()
    near_z, far_z = along_z[:1], along_z[1:]
    return [
        along_x + along_y + near_z + far_z,
        along_y + near_z + along_x + far_z,
        near_z + far_z + along_x + along_y,
        along_x + along_y + near_z + far_z,
    ]


def sum_chunk(parts, core, order):
    rows = parts[0].shape[0] // 2
    own, out = (parts[0][k : k + rows] + parts[1][k : k + rows] for k in (0, rows))
    parts = [own, order[0].send(out)]
    for swap in order[1:-1]:
        own, out = cut(parts, swap)
        parts = [own, swap.send(out)]
    value = parts[0] + parts[1]
    value = value + order[-1].send(value)
    for swap in order[-2:0:-1]:
        value = double(value, swap)
    got = order[0].send(value)
    return [value, got, core.send(value), core.send(got)]


def body(
    hot_table, cold_table, hot_need, cold_need, self_index, neighbors, w_self, w_neigh, cotangent
):
    n_src = hot_need.size + cold_need.size
    counts = count_matrices(neighbors, self_index, n_src)
    core = axis_swaps()[0][0]
    orders = orders_of_sums()
    device = jnp.stack([core.bit, lax.axis_index("dev")] + [order[0].bit for order in orders])
    hot_rows, cold_rows, far_mask = fetch_rows(hot_table, cold_table, hot_need, cold_need, device)
    chunks = CHUNKS // CALLS
    hidden, sums = None, []
    for call in range(CALLS):
        hidden, *grads = layer(
            call,
            chunks,
            far_mask,
            device,
            counts,
            hot_rows,
            cold_rows,
            w_self,
            w_neigh,
            cotangent,
            hidden,
        )
        for keep, send in zip(grads[::2], grads[1::2]):
            sums.append([keep, core.send(send)])
    pieces = []
    for parts, order in zip(sums, orders):
        pieces += sum_chunk(parts, core, order)
    where = jnp.stack([core.bit] + [order[0].bit for order in orders]).astype(jnp.int32)
    grad_self, grad_neigh = place(where, pieces)
    return (hidden, grad_self, grad_neigh)


def solution(mesh):
    in_specs = (
        P("dev", None),
        P(("grp", "dev"), None),
        P(("grp", "dev"), None),
        P(("grp", "dev"), None),
        P(("grp", "dev")),
        P(("grp", "dev"), None),
        P(),
        P(),
        P(("grp", "dev"), None),
    )
    out_specs = (P(("grp", "dev"), None), P(), P())
    return jax.shard_map(body, mesh=mesh, in_specs=in_specs, out_specs=out_specs, check_vma=False)
```
